1024 devices in a mesh: dp: 64 (over x_lo, y, core), fsdp: 16 (over x_hi, z).
Axes of the slice: x: 8 (x_hi: 2, x_lo: 4; x = x_hi * 4 + x_lo), y: 8, z: 8, core: 2. Of those that a mesh axis runs over, the one named last changes fastest.
Arguments:
- shots_in: bfloat16 [8192, 32768], P(('dp', 'fsdp')), may hold values from -24 to 24
- cotangent: bfloat16 [8192, 32768], P(('dp', 'fsdp')), may hold values from -6 to 6
- blocks: bfloat16 [256, 256, 256], P('fsdp'), may hold values from -0.25 to 0.25
- block_rows: int32 [256], replicated, may hold values from 0 to 127, as said below
- block_cols: int32 [256], replicated, may hold values from 0 to 127, as said below
Outputs:
- shots_out: bfloat16 [8192, 32768], P(('dp', 'fsdp'))
- input_grad: bfloat16 [8192, 32768], P(('dp', 'fsdp'))
- weight_grad: float32 [256, 256, 256], P('fsdp', 'dp')
The draws below stay inside these ranges and needn't reach their ends.
Inputs may be any that keep to these rules, and one draw needn't show every extreme that they name: Blocks are stored in runs of 2: blocks 2 * j to 2 * j + 1 share one block row; every block row holds exactly 2 blocks with different block columns; every block column holds at least one block; block_rows and block_cols list the same blocks in the same order. `block_cols`: see block_rows.
All inputs are finite; a program needn't handle non-finite values.
Results may differ from the reference program's by a relative error of at most 0.001.
Values may be sent and summed in bfloat16 or wider, within the bound.
No kernel may reach another device: no remote copies, remote signals or barrier semaphores. Data moves between devices by JAX's collectives and lax.ppermute only.
A program may use at most 32 MiB of HBM per device.

```python
import jax
import jax.numpy as jnp
from jax import lax

BS = 256
RB = 128
PER_ROW = 2
CB = 128
NBLK = 256
SHOTS = 8192


def pattern_pairs(key):
    base = jax.random.fold_in(key, 9173)
    first, second, third = jax.random.split(base, 3)
    shuffled = jax.random.permutation(first, CB).astype(jnp.int32)
    offsets = jax.random.randint(second, (RB,), 1, CB).astype(jnp.int32)
    row_order = jax.random.permutation(third, RB).astype(jnp.int32)
    indices = jnp.arange(NBLK, dtype=jnp.int32)
    rows_list = row_order[indices // PER_ROW]
    cols_list = (shuffled[rows_list] + indices % PER_ROW * offsets[rows_list]) % CB
    return (rows_list.astype(jnp.int32), cols_list.astype(jnp.int32))


def draw_block_rows(key, part):
    return pattern_pairs(key)[0]


def draw_block_cols(key, part):
    return pattern_pairs(key)[1]


def raised(entries, own_key, source, target, shards_of, factor):
    def block_of(axis_at):
        return (jnp.arange(entries.shape[axis_at]) // (entries.shape[axis_at] // shards_of)).reshape((-1,) + (1,) * (entries.ndim - 1 - axis_at))

    near = jax.random.permutation(own_key, shards_of)[block_of(target)]
    second = (block_of(target) + shards_of // 2) % shards_of
    return jnp.where((block_of(source) == near) | (block_of(source) == second), factor * entries, entries)


def block_levels(rng, shape, cuts, smallest, top_value):
    def one(axis_at, blocks):
        heights = jax.random.uniform(jax.random.fold_in(jax.random.fold_in(rng, 6), axis_at), (blocks,), jnp.float32, smallest / len(cuts), top_value / len(cuts))
        return jnp.repeat(jnp.exp(heights), shape[axis_at] // blocks).reshape((-1,) + (1,) * (len(shape) - axis_at - 1))

    factor_of = one(*cuts[0])
    for cut in cuts[1:]:
        factor_of = factor_of * one(*cut)
    return factor_of


def noise(rng, shape, width, most, pieces=(), kind=jnp.bfloat16):
    drawn = jax.random.normal(rng, shape, jnp.float32) * width
    if len(pieces) > 0:
        drawn = block_levels(rng, shape, pieces, -0.22, 0.18) * drawn
    return jnp.clip(drawn, min=-most, max=most).astype(kind)


def bell_draw_with(key, dims, deviation, reach, pieces, heavy, kind=jnp.bfloat16):
    drawn = deviation * jax.random.normal(key, dims, jnp.float32)
    if pieces:
        drawn = drawn * block_levels(key, dims, pieces, -0.22, 0.18)
    return jnp.clip(raised(drawn, jax.random.fold_in(key, 3), *heavy), -reach, reach).astype(kind)


def setup_inputs(seed: int = 0) -> dict:
    seeds = jax.random.split(jax.random.key(seed), 6)
    return {
        "shots_in": bell_draw_with(seeds[0], (SHOTS, CB * BS), 1.0, 24.0, ((0, 1024),), (0, 1, 1024, 6.0)),
        "cotangent": noise(seeds[1], (SHOTS, RB * BS), 1.0, 6.0, ((0, 1024),)),
        "blocks": noise(seeds[2], (NBLK, BS, BS), (PER_ROW * BS) ** -0.5, 0.25, ((0, 16),)),
        "block_rows": draw_block_rows(jax.random.fold_in(seeds[5], 71), 0),
        "block_cols": draw_block_cols(jax.random.fold_in(seeds[5], 71), 0),
    }


def reference(shots_in, cotangent, blocks, block_rows, block_cols):
    inputs = shots_in.reshape(SHOTS, CB, BS)
    grads = cotangent.reshape(SHOTS, RB, BS)
    pairs = jnp.arange(RB, dtype=jnp.int32)

    def row_values(pair):
        total = jnp.zeros((SHOTS, BS), jnp.float32)
        for member in range(PER_ROW):
            position = pair * PER_ROW + member
            col_index = block_cols[position]
            column = lax.dynamic_index_in_dim(inputs, col_index, 1, keepdims=False)
            total = total + jnp.dot(column, blocks[position], preferred_element_type=jnp.float32)
        return total.astype(jnp.bfloat16)

    values = lax.map(row_values, pairs)
    row_of_pair = block_rows[pairs * PER_ROW]
    placed = jnp.zeros((RB, SHOTS, BS), jnp.bfloat16).at[row_of_pair].set(values)
    shots_out = jnp.transpose(placed, (1, 0, 2)).reshape(SHOTS, RB * BS)

    def back_step(running, position):
        row_index = block_rows[position]
        col_index = block_cols[position]
        row_grad = lax.dynamic_index_in_dim(grads, row_index, 1, keepdims=False)
        product = lax.dot_general(row_grad, blocks[position], (((1,), (1,)), ((), ())), preferred_element_type=jnp.float32)
        current = lax.dynamic_index_in_dim(running, col_index, 0, keepdims=False)
        return lax.dynamic_update_index_in_dim(running, current + product, col_index, 0), None

    back = lax.scan(back_step, jnp.zeros((CB, SHOTS, BS), jnp.float32), jnp.arange(NBLK, dtype=jnp.int32))[0]
    input_grad = jnp.transpose(back, (1, 0, 2)).reshape(SHOTS, CB * BS).astype(jnp.bfloat16)

    def grad_block(position):
        column = lax.dynamic_index_in_dim(inputs, block_cols[position], 1, keepdims=False)
        row_grad = lax.dynamic_index_in_dim(grads, block_rows[position], 1, keepdims=False)
        return lax.dot_general(column, row_grad, (((0,), (0,)), ((), ())), preferred_element_type=jnp.float32)

    weight_grad = lax.map(grad_block, jnp.arange(NBLK, dtype=jnp.int32)) * (float(SHOTS) ** -0.5)
    return shots_out, input_grad, weight_grad
```

```python
import functools

import jax
import jax.numpy as jnp
from jax import lax
from jax.experimental import pallas as pl
from jax.experimental.pallas import tpu as pltpu
from jax.sharding import PartitionSpec as P

AXES = ("dp", "fsdp")
XL, Y, CORES, XH, Z = 4, 8, 2, 2, 8
OWNERS = XH * Z
S = 8
B = 256
HALF = 12 * B
MESSAGE = 2 * HALF
SCALES = 128
STEPS = 16.0


def device(xl, y, core, xh, z):
    return (((xl * Y + y) * CORES + core) * XH + xh) * Z + z


def groups():
    return [
        [device((xl + 2 * xh) % XL, y, core, xh, z) for xh in range(XH) for z in range(Z)]
        for xl in range(XL)
        for y in range(Y)
        for core in range(CORES)
    ]


def moves(target):
    return [
        (device(xl, y, core, xh, z), device(*target(xl, y, core), xh, z))
        for xl in range(XL)
        for y in range(Y)
        for core in range(CORES)
        for xh in range(XH)
        for z in range(Z)
    ]


def gather_kernel(cols, rows, x_ref, g_ref, out_ref):
    base = pl.program_id(0) * 4

    @pl.loop(0, 4)
    def _(p):
        for half in range(2):
            for j in range(8):
                col = pl.multiple_of(cols[(base + p) * 16 + half * 8 + j] * B, B)
                at = half * HALF + j * B
                out_ref[p, :, at : at + B] = x_ref[:, pl.ds(col, B)]
            for j in range(4):
                row = pl.multiple_of(rows[(base + p) * 16 + half * 8 + 2 * j] * B, B)
                at = half * HALF + (8 + j) * B
                out_ref[p, :, at : at + B] = g_ref[:, pl.ds(row, B)]


def gather(block_cols, block_rows, shots_in, cotangent):
    return pl.pallas_call(
        gather_kernel,
        out_shape=jax.ShapeDtypeStruct((OWNERS, S, MESSAGE), jnp.bfloat16),
        grid_spec=pltpu.PrefetchScalarGridSpec(
            num_scalar_prefetch=2,
            grid=(4,),
            in_specs=[
                pl.BlockSpec((S, 128 * B), lambda i, c, r: (0, 0)),
                pl.BlockSpec((S, 128 * B), lambda i, c, r: (0, 0)),
            ],
            out_specs=pl.BlockSpec((4, S, MESSAGE), lambda i, c, r: (i, 0, 0)),
        ),
        name="gather",
    )(block_cols, block_rows, shots_in, cotangent)


def fixed(v):
    top = jnp.max(jnp.abs(v), axis=1, keepdims=True)
    e = jnp.ceil(jnp.log2(jnp.maximum(top, 2.0**-120)) * STEPS + 0.01)
    q = v * jnp.exp2(e * (-1.0 / STEPS)) * 32760.0
    return jnp.clip(jnp.round(q), -32767.0, 32767.0), e


def decoded(e):
    return jnp.exp2(e.astype(jnp.int32).astype(jnp.float32) * (1.0 / STEPS)) * (1.0 / 32760.0)


def apply_kernel(x_ref, g_ref, w_ref, out_ref, scale_ref):
    s = pl.program_id(0)
    lanes = lax.broadcasted_iota(jnp.int32, (OWNERS * S, SCALES), 1)
    x = x_ref[...]
    g = g_ref[...]

    def put(slot, v):
        q, e = fixed(v)
        at = pl.multiple_of(s * (3 * B), B) + slot * B
        out_ref[:, pl.ds(at, B)] = q.astype(jnp.int32).astype(jnp.int16)
        scale_ref[...] = jnp.where(lanes == s * 3 + slot, e, scale_ref[...])

    @pl.when(s == 0)
    def _():
        scale_ref[...] = jnp.zeros_like(scale_ref)

    dot = functools.partial(lax.dot_general, preferred_element_type=jnp.float32)
    put(0, dot(x[:, :B], w_ref[0], (((1,), (0,)), ((), ()))) + dot(x[:, B:], w_ref[1], (((1,), (0,)), ((), ()))))
    put(1, dot(g, w_ref[0], (((1,), (1,)), ((), ()))))
    put(2, dot(g, w_ref[1], (((1,), (1,)), ((), ()))))

    @pl.when(s == 7)
    def _():
        out_ref[:, MESSAGE:] = scale_ref[...].astype(jnp.int32).astype(jnp.int16)


def apply(received, blocks):
    shots = OWNERS * S
    return pl.pallas_call(
        apply_kernel,
        out_shape=jax.ShapeDtypeStruct((shots, MESSAGE + SCALES), jnp.int16),
        grid=(8,),
        in_specs=[
            pl.BlockSpec((shots, 2 * B), lambda s: (0, s // 4 * 6 + s % 4)),
            pl.BlockSpec((shots, B), lambda s: (0, s // 4 * 12 + 8 + s % 4)),
            pl.BlockSpec((2, B, B), lambda s: (s, 0, 0)),
        ],
        out_specs=pl.BlockSpec((shots, MESSAGE + SCALES), lambda s: (0, 0)),
        scratch_shapes=[pltpu.VMEM((shots, SCALES), jnp.float32)],
        name="apply",
    )(received, received, blocks)


def grad_kernel(ids, own_ref, other_ref, *refs):
    outs, wg_ref, scale_ref = refs[:Y], refs[Y], refs[Y + 1]
    y = ids[1]
    dot = functools.partial(lax.dot_general, dimension_numbers=(((0,), (0,)), ((), ())), preferred_element_type=jnp.float32)
    lanes = lax.broadcasted_iota(jnp.int32, (B, SCALES), 1)
    scales = jnp.zeros((B, SCALES), jnp.float32)
    for j in range(8):
        a = slice(j * B, (j + 1) * B)
        b = slice((8 + j // 2) * B, (9 + j // 2) * B)
        wg = dot(own_ref[:, a], own_ref[:, b]) + dot(other_ref[:, a], other_ref[:, b])
        q, e = fixed(wg)
        scales = jnp.where(lanes == j, e, scales)
        wg_ref[...] = q.reshape(XL, Y, S, B)
        for d in range(Y):
            part = wg_ref[:, pl.ds(lax.rem(y + d, Y), 1)].reshape(XL * S, B)
            outs[d][:, a] = part.astype(jnp.int32).astype(jnp.int16)
    scale_ref[...] = scales.reshape(XL, Y, S, SCALES)
    for d in range(Y):
        part = scale_ref[:, pl.ds(lax.rem(y + d, Y), 1)].reshape(XL * S, SCALES)
        outs[d][:, 8 * B :] = part.astype(jnp.int32).astype(jnp.int16)


def grad(ids, received, other):
    shots = OWNERS * S
    part = (XL * S, 8 * B + SCALES)
    return pl.pallas_call(
        grad_kernel,
        out_shape=[jax.ShapeDtypeStruct(part, jnp.int16)] * Y,
        grid_spec=pltpu.PrefetchScalarGridSpec(
            num_scalar_prefetch=1,
            grid=(1,),
            in_specs=[
                pl.BlockSpec((shots, HALF), lambda i, ids: (0, ids[0])),
                pl.BlockSpec((shots, HALF), lambda i, ids: (0, 0)),
            ],
            out_specs=[pl.BlockSpec(part, lambda i, ids: (0, 0))] * Y,
            scratch_shapes=[
                pltpu.VMEM((XL, Y, S, B), jnp.float32),
                pltpu.VMEM((XL, Y, S, SCALES), jnp.float32),
            ],
        ),
        name="grad",
    )(ids, received, other)


def sum_kernel(ids, *refs):
    ins, outs, total_ref = refs[:Y], refs[Y : Y + XL], refs[Y + XL]
    xl = ids[2]
    scales = [decoded(ref[:, 8 * B :]) for ref in ins]
    for j in range(8):
        total = jnp.zeros((XL * S, B), jnp.float32)
        for ref, scale in zip(ins, scales):
            q = ref[:, j * B : (j + 1) * B].astype(jnp.int32).astype(jnp.float32)
            total = total + q * scale[:, j : j + 1]
        total_ref[...] = total.reshape(XL, S, B)
        for d in range(XL):
            outs[d][j] = total_ref[lax.rem(xl + d, XL)]


def sum_groups(ids, parts):
    part = (XL * S, 8 * B + SCALES)
    return pl.pallas_call(
        sum_kernel,
        out_shape=[jax.ShapeDtypeStruct((8, S, B), jnp.float32)] * XL,
        grid_spec=pltpu.PrefetchScalarGridSpec(
            num_scalar_prefetch=1,
            grid=(1,),
            in_specs=[pl.BlockSpec(part, lambda i, ids: (0, 0))] * Y,
            out_specs=[pl.BlockSpec((8, S, B), lambda i, ids: (0, 0, 0))] * XL,
            scratch_shapes=[pltpu.VMEM((XL, S, B), jnp.float32)],
        ),
        name="sum_groups",
    )(ids, *parts)


def place_kernel(cols, rows, in_ref, out_ref, grad_ref, total_ref):
    step = pl.program_id(0)

    @pl.when(step == 0)
    def _():
        total_ref[...] = jnp.zeros_like(total_ref)

    @pl.loop(0, 4)
    def _(i):
        p = step * 4 + i
        scale = decoded(in_ref[i, :, MESSAGE:])
        for s in range(8):
            def value(slot):
                at = s * 3 * B + slot * B
                q = in_ref[i, :, at : at + B].astype(jnp.int32).astype(jnp.float32)
                return q * scale[:, s * 3 + slot : s * 3 + slot + 1]

            row = pl.multiple_of(rows[p * 16 + 2 * s] * B, B)
            out_ref[:, pl.ds(row, B)] = value(0).astype(jnp.bfloat16)
            for member in range(2):
                col = pl.multiple_of(cols[p * 16 + 2 * s + member] * B, B)
                total_ref[:, pl.ds(col, B)] += value(1 + member)

    @pl.when(step == 3)
    def _():
        grad_ref[...] = total_ref[...].astype(jnp.bfloat16)


def place(block_cols, block_rows, back):
    return pl.pallas_call(
        place_kernel,
        out_shape=[jax.ShapeDtypeStruct((S, 128 * B), jnp.bfloat16)] * 2,
        grid_spec=pltpu.PrefetchScalarGridSpec(
            num_scalar_prefetch=2,
            grid=(4,),
            in_specs=[pl.BlockSpec((4, S, MESSAGE + SCALES), lambda i, c, r: (i, 0, 0))],
            out_specs=[pl.BlockSpec((S, 128 * B), lambda i, c, r: (0, 0))] * 2,
            scratch_shapes=[pltpu.VMEM((S, 128 * B), jnp.float32)],
        ),
        name="place",
    )(block_cols, block_rows, back)


def shards(shots_in, cotangent, blocks, block_rows, block_cols):
    dp = lax.axis_index("dp")
    core, y, xl = dp % CORES, dp // CORES % Y, dp // (CORES * Y)
    ids = jnp.stack([core, y, xl]).astype(jnp.int32)
    permute = functools.partial(lax.ppermute, axis_name=AXES)
    exchange = functools.partial(
        lax.all_to_all, axis_name=AXES, split_axis=0, concat_axis=0, axis_index_groups=groups(), tiled=True
    )

    received = exchange(gather(block_cols, block_rows, shots_in, cotangent)).reshape(OWNERS * S, MESSAGE)
    theirs = lax.dynamic_slice_in_dim(received, (1 - core) * HALF, HALF, axis=1)
    other = permute(theirs, perm=moves(lambda a, b, c: (a, b, 1 - c)))
    result = apply(received, blocks)
    back = exchange(result.reshape(OWNERS, S, MESSAGE + SCALES))
    parts = grad(ids, received, other)
    parts = [parts[0]] + [
        permute(parts[d], perm=moves(lambda a, b, c, d=d: (a, (b + d) % Y, c))) for d in range(1, Y)
    ]
    sums = sum_groups(ids, parts)
    total = sums[0]
    for d in range(1, XL):
        total = total + permute(sums[d], perm=moves(lambda a, b, c, d=d: ((a + d) % XL, b, c)))
    total = (total * (8192.0**-0.5)).reshape(8, 2, 4, B)
    mine = lax.dynamic_index_in_dim(total, core, 1, keepdims=False)
    swapped = permute(
        lax.dynamic_index_in_dim(total, 1 - core, 1, keepdims=False), perm=moves(lambda a, b, c: (a, b, 1 - c))
    )
    weight_grad = jnp.where(
        core == 0, jnp.concatenate([mine, swapped]), jnp.concatenate([swapped, mine])
    )
    shots_out, input_grad = place(block_cols, block_rows, back)
    return shots_out, input_grad, weight_grad


def solution(mesh):
    return jax.shard_map(
        shards,
        mesh=mesh,
        in_specs=(P(AXES, None), P(AXES, None), P("fsdp", None, None), P(), P()),
        out_specs=(P(AXES, None), P(AXES, None), P("fsdp", "dp", None)),
        check_vma=False,
    )
```

```python
import functools

import jax
import jax.numpy as jnp
from jax import lax
from jax.experimental import pallas as pl
from jax.experimental.pallas import tpu as pltpu
from jax.sharding import PartitionSpec as P

AXES = ("dp", "fsdp")
XL, Y, CORES, XH, Z = 4, 8, 2, 2, 8
OWNERS = XH * Z
S = 8
B = 256
HALF = 12 * B
MESSAGE = 2 * HALF
SCALES = 128
STEPS = 16.0
ROOM = pltpu.CompilerParams(vmem_limit_bytes=24 * 2**20)


def device(xl, y, core, xh, z):
    return (((xl * Y + y) * CORES + core) * XH + xh) * Z + z


def groups():
    return [
        [device((xl + 2 * xh) % XL, y, core, xh, z) for xh in range(XH) for z in range(Z)]
        for xl in range(XL)
        for y in range(Y)
        for core in range(CORES)
    ]


def moves(target):
    return [
        (device(xl, y, core, xh, z), device(*target(xl, y, core), xh, z))
        for xl in range(XL)
        for y in range(Y)
        for core in range(CORES)
        for xh in range(XH)
        for z in range(Z)
    ]


LONG = pl.CostEstimate(flops=20_000_000_000, bytes_accessed=1_000_000, transcendentals=0)


def gather_kernel(cols, rows, x_ref, g_ref, out_ref):
    base = pl.program_id(0) * 4
    for p in range(4):
        for half in range(2):
            first = (base + p) * 16 + half * 8
            for j in range(8):
                col = pl.multiple_of(cols[first + j] * B, B)
                at = half * HALF + j * B
                out_ref[p, :, at : at + B] = x_ref[:, pl.ds(col, B)]
            for j in range(4):
                row = pl.multiple_of(rows[first + 2 * j] * B, B)
                at = half * HALF + (8 + j) * B
                out_ref[p, :, at : at + B] = g_ref[:, pl.ds(row, B)]


def gather(block_cols, block_rows, shots_in, cotangent):
    return pl.pallas_call(
        gather_kernel,
        out_shape=jax.ShapeDtypeStruct((OWNERS, S, MESSAGE), jnp.bfloat16),
        grid_spec=pltpu.PrefetchScalarGridSpec(
            num_scalar_prefetch=2,
            grid=(4,),
            in_specs=[
                pl.BlockSpec((S, 128 * B), lambda i, c, r: (0, 0)),
                pl.BlockSpec((S, 128 * B), lambda i, c, r: (0, 0)),
            ],
            out_specs=pl.BlockSpec((4, S, MESSAGE), lambda i, c, r: (i, 0, 0)),
        ),
        name="gather",
    )(block_cols, block_rows, shots_in, cotangent)


def fixed(v):
    top = jnp.max(jnp.abs(v), axis=1, keepdims=True)
    e = jnp.ceil(jnp.log2(jnp.maximum(top, 2.0**-120)) * STEPS + 0.01)
    return jnp.round(v * (jnp.exp2(e * (-1.0 / STEPS)) * 32760.0)).astype(jnp.int32).astype(jnp.int16), e


def decoded(e):
    return jnp.exp2(e.astype(jnp.int32).astype(jnp.float32) * (1.0 / STEPS)) * (1.0 / 32760.0)


def widened(q):
    return q.astype(jnp.int32).astype(jnp.float32)


def at(j, width=B):
    return slice(j * B, j * B + width)


def dot(u, v, over):
    return lax.dot_general(u, v, (over, ((), ())), preferred_element_type=jnp.float32)


def put_scales(ref, scales):
    lanes = lax.broadcasted_iota(jnp.int32, (scales[0].shape[0], SCALES), 1)
    out = jnp.zeros(lanes.shape, jnp.float32)
    for j, e in enumerate(scales):
        out = jnp.where(lanes == j, e, out)
    ref[:, ref.shape[1] - SCALES :] = out.astype(jnp.int32).astype(jnp.int16)


def grad_kernel(ids, in_ref, other_ref, send_ref, keep_ref, wg_ref):
    core, parity = ids[0], lax.rem(ids[1], 2)
    scales = []
    for j in range(8):
        own = lambda slot: in_ref[:, pl.ds(pl.multiple_of(core * HALF + slot * B, B), B)]
        x0, g0 = own(j), own(8 + j // 2)
        x1, g1 = other_ref[:, at(j)], other_ref[:, at(8 + j // 2)]
        wg = dot(x0, g0, ((0,), (0,))) + dot(x1, g1, ((0,), (0,)))
        wg_ref[...] = wg.reshape(16, 2, S, B)
        keep_ref[:, at(j)] = wg_ref[:, pl.ds(parity, 1)].reshape(128, B)
        q, e = fixed(wg_ref[:, pl.ds(1 - parity, 1)].reshape(128, B))
        send_ref[:, at(j)] = q
        scales.append(e)
    put_scales(send_ref, scales)


def apply_kernel(in_ref, w_ref, after_ref, out_ref):
    scales = []
    for s in range(8):
        first = s // 4 * 12 + s % 4 * 2
        x0, x1, g = in_ref[:, at(first)], in_ref[:, at(first + 1)], in_ref[:, at(s // 4 * 12 + 8 + s % 4)]
        w0, w1 = w_ref[2 * s], w_ref[2 * s + 1]
        values = (
            dot(x0, w0, ((1,), (0,))) + dot(x1, w1, ((1,), (0,))),
            dot(g, w0, ((1,), (1,))),
            dot(g, w1, ((1,), (1,))),
        )
        for slot, value in enumerate(values):
            q, e = fixed(value)
            out_ref[:, at(3 * s + slot)] = q
            scales.append(e)
    put_scales(out_ref, scales)


def here(*arrays):
    return [pltpu.with_memory_space_constraint(a, pltpu.VMEM) for a in arrays]


def vmem(n):
    return [pl.BlockSpec(memory_space=pltpu.VMEM)] * n


SMEM = pl.BlockSpec(memory_space=pltpu.SMEM)
PART = 8 * B + SCALES


def grad(ids, received, other):
    return pl.pallas_call(
        grad_kernel,
        out_shape=[pltpu.VMEM((128, PART), jnp.int16), pltpu.VMEM((128, 8 * B), jnp.float32)],
        in_specs=[SMEM] + vmem(2),
        out_specs=vmem(2),
        scratch_shapes=[pltpu.VMEM((16, 2, S, B), jnp.float32)],
        compiler_params=ROOM,
        name="grad",
    )(ids, *here(received, other))


def apply(received, blocks, after):
    return pl.pallas_call(
        apply_kernel,
        out_shape=jax.ShapeDtypeStruct((OWNERS * S, MESSAGE + SCALES), jnp.int16),
        in_specs=vmem(3),
        compiler_params=ROOM,
        cost_estimate=pl.CostEstimate(flops=5_000_000_000, bytes_accessed=20_000_000, transcendentals=0),
        name="apply",
    )(*here(received, blocks, after))


def pairs_kernel(ids, keep_ref, got_ref, *refs):
    outs, own_ref, total_ref = refs[:3], refs[3], refs[4]
    pair = ids[1] // 2
    scale = decoded(got_ref[:, 8 * B :])
    scales = [[] for _ in range(3)]
    for j in range(8):
        total = keep_ref[:, at(j)] + widened(got_ref[:, at(j)]) * scale[:, j : j + 1]
        total_ref[...] = total.reshape(XL, 4, S, B)
        own_ref[:, at(j)] = total_ref[:, pl.ds(pair, 1)].reshape(32, B)
        for d in range(3):
            q, e = fixed(total_ref[:, pl.ds(lax.rem(pair + d + 1, 4), 1)].reshape(32, B))
            outs[d][:, at(j)] = q
            scales[d].append(e)
    for d in range(3):
        put_scales(outs[d], scales[d])


def pairs(ids, keep, got):
    return pl.pallas_call(
        pairs_kernel,
        out_shape=[pltpu.VMEM((32, PART), jnp.int16)] * 3
        + [pltpu.VMEM((32, 8 * B), jnp.float32)],
        in_specs=[SMEM] + vmem(2),
        out_specs=vmem(4),
        scratch_shapes=[pltpu.VMEM((XL, 4, S, B), jnp.float32)],
        compiler_params=ROOM,
        cost_estimate=LONG,
        name="pairs",
    )(ids, *here(keep, got))


def halves_kernel(ids, own_ref, a_ref, b_ref, c_ref, keep_ref, send_ref, total_ref):
    parity = lax.rem(ids[2], 2)
    ins = (a_ref, b_ref, c_ref)
    scales = [decoded(ref[:, 8 * B :]) for ref in ins]
    for j in range(8):
        total = own_ref[:, at(j)]
        for ref, scale in zip(ins, scales):
            total = total + widened(ref[:, at(j)]) * scale[:, j : j + 1]
        total_ref[...] = total.reshape(2, 2, S, B)
        keep_ref[:, at(j)] = total_ref[:, pl.ds(parity, 1)].reshape(16, B)
        send_ref[:, at(j)] = total_ref[:, pl.ds(1 - parity, 1)].reshape(16, B)


def halves(ids, own, parts):
    return pl.pallas_call(
        halves_kernel,
        out_shape=[pltpu.VMEM((16, 8 * B), jnp.float32)] * 2,
        in_specs=[SMEM] + vmem(4),
        out_specs=vmem(2),
        scratch_shapes=[pltpu.VMEM((2, 2, S, B), jnp.float32)],
        compiler_params=ROOM,
        name="halves",
    )(ids, *here(own, *parts))


def place_kernel(cols, rows, in_ref, out_ref, grad_ref, first_ref, second_ref):
    totals = (first_ref, second_ref)
    for ref in totals:
        ref[...] = jnp.zeros_like(ref)

    @pl.loop(0, OWNERS)
    def _(p):
        scale = decoded(in_ref[p, :, MESSAGE:])
        values = [widened(in_ref[p, :, at(j)]) * scale[:, j : j + 1] for j in range(24)]
        for s in range(8):
            row = pl.multiple_of(rows[p * 16 + 2 * s] * B, B)
            out_ref[:, pl.ds(row, B)] = values[3 * s].astype(jnp.bfloat16)
            for member, ref in enumerate(totals):
                col = pl.multiple_of(cols[p * 16 + 2 * s + member] * B, B)
                ref[:, pl.ds(col, B)] += values[3 * s + 1 + member]

    grad_ref[...] = (first_ref[...] + second_ref[...]).astype(jnp.bfloat16)


def place(block_cols, block_rows, back):
    return pl.pallas_call(
        place_kernel,
        out_shape=[jax.ShapeDtypeStruct((S, 128 * B), jnp.bfloat16)] * 2,
        in_specs=[SMEM, SMEM] + vmem(1),
        scratch_shapes=[pltpu.VMEM((S, 128 * B), jnp.float32)] * 2,
        compiler_params=ROOM,
        name="place",
    )(block_cols, block_rows, *here(back))


def shards(shots_in, cotangent, blocks, block_rows, block_cols):
    dp = lax.axis_index("dp")
    core, y, xl = dp % CORES, dp // CORES % Y, dp // (CORES * Y)
    ids = jnp.stack([core, y, xl]).astype(jnp.int32)
    permute = functools.partial(lax.ppermute, axis_name=AXES)
    exchange = functools.partial(
        lax.all_to_all, axis_name=AXES, split_axis=0, concat_axis=0, axis_index_groups=groups(), tiled=True
    )

    received = exchange(gather(block_cols, block_rows, shots_in, cotangent)).reshape(OWNERS * S, MESSAGE)
    theirs = lax.dynamic_slice_in_dim(received, (1 - core) * HALF, HALF, axis=1)
    other = permute(theirs, perm=moves(lambda a, b, c: (a, b, 1 - c)))
    send, keep = grad(ids, received, other)
    result = apply(received, blocks, keep)
    got = permute(send, perm=moves(lambda a, b, c: (a, b ^ 1, c)))
    back = exchange(result.reshape(OWNERS, S, MESSAGE + SCALES))
    *parts, own = pairs(ids, keep, got)
    parts = [
        permute(part, perm=moves(lambda a, b, c, d=d: (a, (b + 2 * d + 2) % Y, c))) for d, part in enumerate(parts)
    ]
    keep, send = halves(ids, own, parts)
    total = keep + permute(send, perm=moves(lambda a, b, c: (a ^ 1, b, c)))
    total = total.reshape(2, S, 8 * B)
    send = lax.dynamic_index_in_dim(total, 1 - xl // 2, 0, keepdims=False)
    total = lax.dynamic_index_in_dim(total, xl // 2, 0, keepdims=False)
    total = total + permute(send, perm=moves(lambda a, b, c: (a ^ 2, b, c)))
    total = (total * (8192.0**-0.5)).reshape(2, 4, 8, B)
    mine = lax.dynamic_index_in_dim(total, core, 0, keepdims=False)
    swapped = permute(
        lax.dynamic_index_in_dim(total, 1 - core, 0, keepdims=False), perm=moves(lambda a, b, c: (a, b, 1 - c))
    )
    weight_grad = jnp.where(
        core == 0, jnp.concatenate([mine, swapped], axis=1), jnp.concatenate([swapped, mine], axis=1)
    ).transpose(1, 0, 2)
    shots_out, input_grad = place(block_cols, block_rows, back)
    return shots_out, input_grad, weight_grad


def solution(mesh):
    return jax.shard_map(
        shards,
        mesh=mesh,
        in_specs=(P(AXES, None), P(AXES, None), P("fsdp", None, None), P(), P()),
        out_specs=(P(AXES, None), P(AXES, None), P("fsdp", "dp", None)),
        check_vma=False,
    )
```

```python
import functools

import jax
import jax.numpy as jnp
from jax import lax
from jax.experimental import pallas as pl
from jax.experimental.pallas import tpu as pltpu
from jax.sharding import PartitionSpec as P

AXES = ("dp", "fsdp")
XL, Y, CORES, XH, Z = 4, 8, 2, 2, 8
OWNERS = XH * Z
S = 8
B = 256
HALF = 12 * B
MESSAGE = 2 * HALF
SCALES = 128
STEPS = 16.0
PAIR_STEPS = (1, 3, 2)
ROOM = pltpu.CompilerParams(vmem_limit_bytes=24 * 2**20)


def device(xl, y, core, xh, z):
    return (((xl * Y + y) * CORES + core) * XH + xh) * Z + z


def groups():
    return [
        [device((xl + 2 * xh) % XL, y, core, xh, z) for xh in range(XH) for z in range(Z)]
        for xl in range(XL)
        for y in range(Y)
        for core in range(CORES)
    ]


def moves(target):
    return [
        (device(xl, y, core, xh, z), device(*target(xl, y, core), xh, z))
        for xl in range(XL)
        for y in range(Y)
        for core in range(CORES)
        for xh in range(XH)
        for z in range(Z)
    ]


LONG = pl.CostEstimate(flops=80_000_000_000, bytes_accessed=1_000_000, transcendentals=0)


def gather_kernel(cols, rows, x_ref, g_ref, out_ref):
    base = pl.program_id(0) * 4
    for p in range(4):
        for half in range(2):
            first = (base + p) * 16 + half * 8
            for j in range(8):
                col = pl.multiple_of(cols[first + j] * B, B)
                at = half * HALF + j * B
                out_ref[p, :, at : at + B] = x_ref[:, pl.ds(col, B)]
            for j in range(4):
                row = pl.multiple_of(rows[first + 2 * j] * B, B)
                at = half * HALF + (8 + j) * B
                out_ref[p, :, at : at + B] = g_ref[:, pl.ds(row, B)]


def gather(block_cols, block_rows, shots_in, cotangent):
    return pl.pallas_call(
        gather_kernel,
        out_shape=jax.ShapeDtypeStruct((OWNERS, S, MESSAGE), jnp.bfloat16),
        grid_spec=pltpu.PrefetchScalarGridSpec(
            num_scalar_prefetch=2,
            grid=(4,),
            in_specs=[
                pl.BlockSpec((S, 128 * B), lambda i, c, r: (0, 0)),
                pl.BlockSpec((S, 128 * B), lambda i, c, r: (0, 0)),
            ],
            out_specs=pl.BlockSpec((4, S, MESSAGE), lambda i, c, r: (i, 0, 0)),
        ),
        name="gather",
    )(block_cols, block_rows, shots_in, cotangent)


def fixed(v):
    top = jnp.max(jnp.abs(v), axis=1, keepdims=True)
    e = jnp.ceil(jnp.log2(jnp.maximum(top, 2.0**-120)) * STEPS + 0.01)
    return jnp.round(v * (jnp.exp2(e * (-1.0 / STEPS)) * 32760.0)).astype(jnp.int32).astype(jnp.int16), e


def decoded(e):
    return jnp.exp2(e.astype(jnp.int32).astype(jnp.float32) * (1.0 / STEPS)) * (1.0 / 32760.0)


def widened(q):
    return q.astype(jnp.int32).astype(jnp.float32)


def at(j, width=B):
    return slice(j * B, j * B + width)


def dot(u, v, over):
    return lax.dot_general(u, v, (over, ((), ())), preferred_element_type=jnp.float32)


def put_scales(ref, scales):
    lanes = lax.broadcasted_iota(jnp.int32, (scales[0].shape[0], SCALES), 1)
    out = jnp.zeros(lanes.shape, jnp.float32)
    for j, e in enumerate(scales):
        out = jnp.where(lanes == j, e, out)
    ref[:, ref.shape[1] - SCALES :] = out.astype(jnp.int32).astype(jnp.int16)


def grad_kernel(ids, in_ref, other_ref, send_ref, keep_ref, wg_ref):
    core, parity = ids[0], lax.rem(ids[1], 2)
    scales = []
    for j in range(8):
        own = lambda slot: in_ref[:, pl.ds(pl.multiple_of(core * HALF + slot * B, B), B)]
        x0, g0 = own(j), own(8 + j // 2)
        x1, g1 = other_ref[:, at(j)], other_ref[:, at(8 + j // 2)]
        wg = dot(x0, g0, ((0,), (0,))) + dot(x1, g1, ((0,), (0,)))
        wg_ref[...] = wg.reshape(16, 2, S, B)
        keep_ref[:, at(j)] = wg_ref[:, pl.ds(parity, 1)].reshape(128, B)
        q, e = fixed(wg_ref[:, pl.ds(1 - parity, 1)].reshape(128, B))
        send_ref[:, at(j)] = q
        scales.append(e)
    put_scales(send_ref, scales)


def apply_kernel(in_ref, w_ref, after_ref, out_ref):
    scales = []
    for s in range(8):
        first = s // 4 * 12 + s % 4 * 2
        x0, x1, g = in_ref[:, at(first)], in_ref[:, at(first + 1)], in_ref[:, at(s // 4 * 12 + 8 + s % 4)]
        w0, w1 = w_ref[2 * s], w_ref[2 * s + 1]
        values = (
            dot(x0, w0, ((1,), (0,))) + dot(x1, w1, ((1,), (0,))),
            dot(g, w0, ((1,), (1,))),
            dot(g, w1, ((1,), (1,))),
        )
        for slot, value in enumerate(values):
            q, e = fixed(value)
            out_ref[:, at(3 * s + slot)] = q
            scales.append(e)
    put_scales(out_ref, scales)


def here(*arrays):
    return [pltpu.with_memory_space_constraint(a, pltpu.VMEM) for a in arrays]


def vmem(n):
    return [pl.BlockSpec(memory_space=pltpu.VMEM)] * n


SMEM = pl.BlockSpec(memory_space=pltpu.SMEM)
PART = 8 * B + SCALES


def grad(ids, received, other):
    return pl.pallas_call(
        grad_kernel,
        out_shape=[pltpu.VMEM((128, PART), jnp.int16), pltpu.VMEM((128, 8 * B), jnp.float32)],
        in_specs=[SMEM] + vmem(2),
        out_specs=vmem(2),
        scratch_shapes=[pltpu.VMEM((16, 2, S, B), jnp.float32)],
        compiler_params=ROOM,
        name="grad",
    )(ids, *here(received, other))


def apply(received, blocks, after):
    return pl.pallas_call(
        apply_kernel,
        out_shape=jax.ShapeDtypeStruct((OWNERS * S, MESSAGE + SCALES), jnp.int16),
        in_specs=vmem(3),
        compiler_params=ROOM,
        cost_estimate=pl.CostEstimate(flops=5_000_000_000, bytes_accessed=20_000_000, transcendentals=0),
        name="apply",
    )(*here(received, blocks, after))


def pairs_kernel(ids, keep_ref, got_ref, *refs):
    outs, own_ref, total_ref = refs[:3], refs[3], refs[4]
    pair = ids[1] // 2
    scale = decoded(got_ref[:, 8 * B :])
    scales = [[] for _ in range(3)]
    for j in range(8):
        total = keep_ref[:, at(j)] + widened(got_ref[:, at(j)]) * scale[:, j : j + 1]
        total_ref[...] = total.reshape(XL, 4, S, B)
        own_ref[:, at(j)] = total_ref[:, pl.ds(pair, 1)].reshape(32, B)
        for d in range(3):
            q, e = fixed(total_ref[:, pl.ds(lax.rem(pair + PAIR_STEPS[d], 4), 1)].reshape(32, B))
            outs[d][:, at(j)] = q
            scales[d].append(e)
    for d in range(3):
        put_scales(outs[d], scales[d])


def pairs(ids, keep, got):
    return pl.pallas_call(
        pairs_kernel,
        out_shape=[pltpu.VMEM((32, PART), jnp.int16)] * 3
        + [pltpu.VMEM((32, 8 * B), jnp.float32)],
        in_specs=[SMEM] + vmem(2),
        out_specs=vmem(4),
        scratch_shapes=[pltpu.VMEM((XL, 4, S, B), jnp.float32)],
        compiler_params=ROOM,
        cost_estimate=LONG,
        name="pairs",
    )(ids, *here(keep, got))


def cut_kernel(ids, own_ref, a_ref, b_ref, c_ref, *refs):
    outs, keep_ref, total_ref = refs[:3], refs[3], refs[4]
    xl = ids[2]
    ins = (a_ref, b_ref, c_ref)
    before = [decoded(ref[:, 8 * B :]) for ref in ins]
    scales = [[] for _ in range(3)]
    for j in range(8):
        total = own_ref[:, at(j)]
        for ref, scale in zip(ins, before):
            total = total + widened(ref[:, at(j)]) * scale[:, j : j + 1]
        total_ref[...] = total.reshape(XL, S, B)
        keep_ref[:, at(j)] = total_ref[xl]
        for d in range(3):
            q, e = fixed(total_ref[xl ^ (d + 1)])
            outs[d][:, at(j)] = q
            scales[d].append(e)
    for d in range(3):
        put_scales(outs[d], scales[d])


def cut(ids, own, parts):
    return pl.pallas_call(
        cut_kernel,
        out_shape=[pltpu.VMEM((S, PART), jnp.int16)] * 3 + [pltpu.VMEM((S, 8 * B), jnp.float32)],
        in_specs=[SMEM] + vmem(4),
        out_specs=vmem(4),
        scratch_shapes=[pltpu.VMEM((XL, S, B), jnp.float32)],
        compiler_params=ROOM,
        name="cut",
    )(ids, *here(own, *parts))


def last_kernel(ids, own_ref, a_ref, b_ref, c_ref, mine_ref, send_ref):
    ins = (a_ref, b_ref, c_ref)
    scales = [decoded(ref[:, 8 * B :]) for ref in ins]
    first = ids[0] == 0
    for j in range(8):
        total = own_ref[:, at(j)]
        for ref, scale in zip(ins, scales):
            total = total + widened(ref[:, at(j)]) * scale[:, j : j + 1]
        total = total * 8192.0**-0.5
        top, bottom = total[:4], total[4:]
        mine_ref[j] = jnp.where(first, top, bottom)
        send_ref[j] = jnp.where(first, bottom, top)


def last(ids, own, parts):
    return pl.pallas_call(
        last_kernel,
        out_shape=[pltpu.VMEM((8, 4, B), jnp.float32)] * 2,
        in_specs=[SMEM] + vmem(4),
        out_specs=vmem(2),
        compiler_params=ROOM,
        name="last",
    )(ids, *here(own, *parts))


def place_kernel(cols, rows, in_ref, out_ref, grad_ref, first_ref, second_ref):
    totals = (first_ref, second_ref)
    for ref in totals:
        ref[...] = jnp.zeros_like(ref)

    @pl.loop(0, OWNERS)
    def _(p):
        scale = decoded(in_ref[p, :, MESSAGE:])
        values = [widened(in_ref[p, :, at(j)]) * scale[:, j : j + 1] for j in range(24)]
        for s in range(8):
            row = pl.multiple_of(rows[p * 16 + 2 * s] * B, B)
            out_ref[:, pl.ds(row, B)] = values[3 * s].astype(jnp.bfloat16)
            for member, ref in enumerate(totals):
                col = pl.multiple_of(cols[p * 16 + 2 * s + member] * B, B)
                ref[:, pl.ds(col, B)] += values[3 * s + 1 + member]

    grad_ref[...] = (first_ref[...] + second_ref[...]).astype(jnp.bfloat16)


def place(block_cols, block_rows, back):
    return pl.pallas_call(
        place_kernel,
        out_shape=[jax.ShapeDtypeStruct((S, 128 * B), jnp.bfloat16)] * 2,
        in_specs=[SMEM, SMEM] + vmem(1),
        scratch_shapes=[pltpu.VMEM((S, 128 * B), jnp.float32)] * 2,
        compiler_params=ROOM,
        name="place",
    )(block_cols, block_rows, *here(back))


def shards(shots_in, cotangent, blocks, block_rows, block_cols):
    dp = lax.axis_index("dp")
    core, y, xl = dp % CORES, dp // CORES % Y, dp // (CORES * Y)
    ids = jnp.stack([core, y, xl]).astype(jnp.int32)
    permute = functools.partial(lax.ppermute, axis_name=AXES)
    exchange = functools.partial(
        lax.all_to_all, axis_name=AXES, split_axis=0, concat_axis=0, axis_index_groups=groups(), tiled=True
    )

    received = exchange(gather(block_cols, block_rows, shots_in, cotangent)).reshape(OWNERS * S, MESSAGE)
    theirs = lax.dynamic_slice_in_dim(received, (1 - core) * HALF, HALF, axis=1)
    other = permute(theirs, perm=moves(lambda a, b, c: (a, b, 1 - c)))
    send, keep = grad(ids, received, other)
    result = apply(received, blocks, keep)
    got = permute(send, perm=moves(lambda a, b, c: (a, b ^ 1, c)))
    back = exchange(result.reshape(OWNERS, S, MESSAGE + SCALES))
    *parts, own = pairs(ids, keep, got)
    parts = [
        permute(part, perm=moves(lambda a, b, c, d=d: (a, (b + 2 * d) % Y, c))) for d, part in zip(PAIR_STEPS, parts)
    ]
    *parts, own = cut(ids, own, parts)
    parts = [
        permute(part, perm=moves(lambda a, b, c, d=d: (a ^ (d + 1), b, c))) for d, part in enumerate(parts)
    ]
    mine, send = last(ids, own, parts)
    swapped = permute(send, perm=moves(lambda a, b, c: (a, b, 1 - c)))
    weight_grad = jnp.where(core == 0, jnp.concatenate([mine, swapped]), jnp.concatenate([swapped, mine]))
    shots_out, input_grad = place(block_cols, block_rows, back)
    return shots_out, input_grad, weight_grad


def solution(mesh):
    return jax.shard_map(
        shards,
        mesh=mesh,
        in_specs=(P(AXES, None), P(AXES, None), P("fsdp", None, None), P(), P()),
        out_specs=(P(AXES, None), P(AXES, None), P("fsdp", "dp", None)),
        check_vma=False,
    )
```

```python
import functools

import jax
import jax.numpy as jnp
from jax import lax
from jax.experimental import pallas as pl
from jax.experimental.pallas import tpu as pltpu
from jax.sharding import PartitionSpec as P

AXES = ("dp", "fsdp")
XL, Y, CORES, XH, Z = 4, 8, 2, 2, 8
OWNERS = XH * Z
S = 8
B = 256
HALF = 12 * B
MESSAGE = 2 * HALF
SCALES = 128
STEPS = 16.0
PAIR_STEPS = (1, 3, 2)
SMEM = pl.BlockSpec(memory_space=pltpu.SMEM)
ANY = pl.BlockSpec(memory_space=pl.ANY)
ROOM = pltpu.CompilerParams(vmem_limit_bytes=24 * 2**20)


def device(xl, y, core, xh, z):
    return (((xl * Y + y) * CORES + core) * XH + xh) * Z + z


def position():
    dp = lax.axis_index("dp")
    return lax.rem(dp, CORES), lax.rem(lax.div(dp, CORES), Y), lax.div(dp, CORES * Y)


def groups():
    return [
        [device((xl + 2 * xh) % XL, y, core, xh, z) for xh in range(XH) for z in range(Z)]
        for xl in range(XL)
        for y in range(Y)
        for core in range(CORES)
    ]


def moves(target):
    return [
        (device(xl, y, core, xh, z), device(*target(xl, y, core), xh, z))
        for xl in range(XL)
        for y in range(Y)
        for core in range(CORES)
        for xh in range(XH)
        for z in range(Z)
    ]


LONG = pl.CostEstimate(flops=80_000_000_000, bytes_accessed=1_000_000, transcendentals=0)


def gather_kernel(cols, rows, x_hbm, g_hbm, out_hbm, x_ref, g_ref, out_ref, in_sems, out_sems):
    loads = [
        pltpu.make_async_copy(x_hbm, x_ref, in_sems.at[0]),
        pltpu.make_async_copy(g_hbm, g_ref, in_sems.at[1]),
    ]
    for load in loads:
        load.start()
    for load in loads:
        load.wait()
    stores = []
    for chunk in range(4):
        owners = slice(chunk * 4, chunk * 4 + 4)
        for p in range(owners.start, owners.stop):
            for half in range(2):
                first = p * 16 + half * 8
                for j in range(8):
                    col = pl.multiple_of(cols[first + j] * B, B)
                    out_ref[p, :, at(half * 12 + j)] = x_ref[:, pl.ds(col, B)]
                for j in range(4):
                    row = pl.multiple_of(rows[first + 2 * j] * B, B)
                    out_ref[p, :, at(half * 12 + 8 + j)] = g_ref[:, pl.ds(row, B)]
        stores.append(pltpu.make_async_copy(out_ref.at[owners], out_hbm.at[owners], out_sems.at[chunk]))
        stores[-1].start()
    for store in stores:
        store.wait()


def gather(block_cols, block_rows, shots_in, cotangent):
    message = (OWNERS, S, MESSAGE)
    return pl.pallas_call(
        gather_kernel,
        out_shape=jax.ShapeDtypeStruct(message, jnp.bfloat16),
        in_specs=[SMEM, SMEM, ANY, ANY],
        out_specs=ANY,
        scratch_shapes=[pltpu.VMEM((S, 128 * B), jnp.bfloat16)] * 2
        + [
            pltpu.VMEM(message, jnp.bfloat16),
            pltpu.SemaphoreType.DMA((2,)),
            pltpu.SemaphoreType.DMA((4,)),
        ],
        name="gather",
    )(block_cols, block_rows, shots_in, cotangent)


def fixed(v):
    top = jnp.max(jnp.abs(v), axis=1, keepdims=True)
    e = jnp.ceil(jnp.log2(jnp.maximum(top, 2.0**-120)) * STEPS + 0.01)
    return jnp.round(v * (jnp.exp2(e * (-1.0 / STEPS)) * 32760.0)).astype(jnp.int32).astype(jnp.int16), e


def decoded(e):
    return jnp.exp2(e.astype(jnp.int32).astype(jnp.float32) * (1.0 / STEPS)) * (1.0 / 32760.0)


def widened(q):
    return q.astype(jnp.int32).astype(jnp.float32)


def at(j, width=B):
    return slice(j * B, j * B + width)


def dot(u, v, over):
    return lax.dot_general(u, v, (over, ((), ())), preferred_element_type=jnp.float32)


def put_scales(ref, scales):
    lanes = lax.broadcasted_iota(jnp.int32, (scales[0].shape[0], SCALES), 1)
    out = jnp.zeros(lanes.shape, jnp.float32)
    for j, e in enumerate(scales):
        out = jnp.where(lanes == j, e, out)
    ref[:, ref.shape[1] - SCALES :] = out.astype(jnp.int32).astype(jnp.int16)


def grad_kernel(in_ref, other_ref, after_ref, send_ref, keep_ref, wg_ref):
    core, y, _ = position()
    parity = y % 2
    scales = []
    for j in range(8):
        own = lambda slot: in_ref[:, pl.ds(pl.multiple_of(core * HALF + slot * B, B), B)]
        x0, g0 = own(j), own(8 + j // 2)
        x1, g1 = other_ref[:, at(j)], other_ref[:, at(8 + j // 2)]
        wg = dot(x0, g0, ((0,), (0,))) + dot(x1, g1, ((0,), (0,)))
        wg_ref[...] = wg.reshape(16, 2, S, B)
        keep_ref[:, at(j)] = wg_ref[:, pl.ds(parity, 1)].reshape(128, B)
        q, e = fixed(wg_ref[:, pl.ds(1 - parity, 1)].reshape(128, B))
        send_ref[:, at(j)] = q
        scales.append(e)
    put_scales(send_ref, scales)


def apply_kernel(in_ref, w_hbm, out_ref, w_ref, sems):
    loads = [
        pltpu.make_async_copy(w_hbm.at[2 * s : 2 * s + 2], w_ref.at[2 * s : 2 * s + 2], sems.at[s]) for s in range(8)
    ]
    for load in loads:
        load.start()
    scales = []
    for s in range(8):
        loads[s].wait()
        first = s // 4 * 12 + s % 4 * 2
        x0, x1, g = in_ref[:, at(first)], in_ref[:, at(first + 1)], in_ref[:, at(s // 4 * 12 + 8 + s % 4)]
        w0, w1 = w_ref[2 * s], w_ref[2 * s + 1]
        values = (
            dot(x0, w0, ((1,), (0,))) + dot(x1, w1, ((1,), (0,))),
            dot(g, w0, ((1,), (1,))),
            dot(g, w1, ((1,), (1,))),
        )
        for slot, value in enumerate(values):
            q, e = fixed(value)
            out_ref[:, at(3 * s + slot)] = q
            scales.append(e)
    put_scales(out_ref, scales)


def here(*arrays):
    return [pltpu.with_memory_space_constraint(a, pltpu.VMEM) for a in arrays]


def vmem(n):
    return [pl.BlockSpec(memory_space=pltpu.VMEM)] * n


PART = 8 * B + SCALES


def grad(received, other, after):
    return pl.pallas_call(
        grad_kernel,
        out_shape=[pltpu.VMEM((128, PART), jnp.int16), pltpu.VMEM((128, 8 * B), jnp.float32)],
        in_specs=vmem(2) + [ANY],
        out_specs=vmem(2),
        scratch_shapes=[pltpu.VMEM((16, 2, S, B), jnp.float32)],
        compiler_params=ROOM,
        name="grad",
    )(*here(received, other), after)


def apply(received, blocks):
    return pl.pallas_call(
        apply_kernel,
        out_shape=jax.ShapeDtypeStruct((OWNERS * S, MESSAGE + SCALES), jnp.int16),
        in_specs=vmem(1) + [ANY],
        scratch_shapes=[pltpu.VMEM((16, B, B), jnp.bfloat16), pltpu.SemaphoreType.DMA((8,))],
        compiler_params=ROOM,
        cost_estimate=pl.CostEstimate(flops=5_000_000_000, bytes_accessed=20_000_000, transcendentals=0),
        name="apply",
    )(*here(received), pltpu.with_memory_space_constraint(blocks, pltpu.HBM))


def pairs_kernel(keep_ref, got_ref, *refs):
    outs, own_ref, total_ref = refs[:3], refs[3], refs[4]
    pair = position()[1] // 2
    scale = decoded(got_ref[:, 8 * B :])
    scales = [[] for _ in range(3)]
    for j in range(8):
        total = keep_ref[:, at(j)] + widened(got_ref[:, at(j)]) * scale[:, j : j + 1]
        total_ref[...] = total.reshape(XL, 4, S, B)
        own_ref[:, at(j)] = total_ref[:, pl.ds(pair, 1)].reshape(32, B)
        for d in range(3):
            q, e = fixed(total_ref[:, pl.ds(lax.rem(pair + PAIR_STEPS[d], 4), 1)].reshape(32, B))
            outs[d][:, at(j)] = q
            scales[d].append(e)
    for d in range(3):
        put_scales(outs[d], scales[d])


def pairs(keep, got):
    return pl.pallas_call(
        pairs_kernel,
        out_shape=[pltpu.VMEM((32, PART), jnp.int16)] * 3
        + [pltpu.VMEM((32, 8 * B), jnp.float32)],
        in_specs=vmem(2),
        out_specs=vmem(4),
        scratch_shapes=[pltpu.VMEM((XL, 4, S, B), jnp.float32)],
        compiler_params=ROOM,
        cost_estimate=LONG,
        name="pairs",
    )(*here(keep, got))


def cut_kernel(own_ref, a_ref, b_ref, c_ref, *refs):
    outs, keep_ref, total_ref = refs[:3], refs[3], refs[4]
    xl = position()[2]
    ins = (a_ref, b_ref, c_ref)
    before = [decoded(ref[:, 8 * B :]) for ref in ins]
    scales = [[] for _ in range(3)]
    for j in range(8):
        total = own_ref[:, at(j)]
        for ref, scale in zip(ins, before):
            total = total + widened(ref[:, at(j)]) * scale[:, j : j + 1]
        total_ref[...] = total.reshape(XL, S, B)
        keep_ref[:, at(j)] = total_ref[xl]
        for d in range(3):
            q, e = fixed(total_ref[xl ^ (d + 1)])
            outs[d][:, at(j)] = q
            scales[d].append(e)
    for d in range(3):
        put_scales(outs[d], scales[d])


def cut(own, parts):
    return pl.pallas_call(
        cut_kernel,
        out_shape=[pltpu.VMEM((S, PART), jnp.int16)] * 3 + [pltpu.VMEM((S, 8 * B), jnp.float32)],
        in_specs=vmem(4),
        out_specs=vmem(4),
        scratch_shapes=[pltpu.VMEM((XL, S, B), jnp.float32)],
        compiler_params=ROOM,
        name="cut",
    )(*here(own, *parts))


def last_kernel(own_ref, a_ref, b_ref, c_ref, after_ref, mine_ref, send_ref):
    ins = (a_ref, b_ref, c_ref)
    scales = [decoded(ref[:, 8 * B :]) for ref in ins]
    first = position()[0] == 0
    for j in range(8):
        total = own_ref[:, at(j)]
        for ref, scale in zip(ins, scales):
            total = total + widened(ref[:, at(j)]) * scale[:, j : j + 1]
        total = total * 8192.0**-0.5
        top, bottom = total[:4], total[4:]
        mine_ref[j] = jnp.where(first, top, bottom)
        send_ref[j] = jnp.where(first, bottom, top)


def last(own, parts, after):
    return pl.pallas_call(
        last_kernel,
        out_shape=[pltpu.VMEM((8, 4, B), jnp.float32)] * 2,
        in_specs=vmem(5),
        out_specs=vmem(2),
        compiler_params=ROOM,
        name="last",
    )(*here(own, *parts, after))


def place_kernel(cols, rows, in_ref, out_ref, grad_ref, mark_ref, first_ref, second_ref):
    mark_ref[...] = jnp.zeros_like(mark_ref)
    totals = (first_ref, second_ref)
    for ref in totals:
        ref[...] = jnp.zeros_like(ref)

    @pl.loop(0, OWNERS)
    def _(p):
        scale = decoded(in_ref[p, :, MESSAGE:])
        values = [widened(in_ref[p, :, at(j)]) * scale[:, j : j + 1] for j in range(24)]
        for s in range(8):
            row = pl.multiple_of(rows[p * 16 + 2 * s] * B, B)
            out_ref[:, pl.ds(row, B)] = values[3 * s].astype(jnp.bfloat16)
            for member, ref in enumerate(totals):
                col = pl.multiple_of(cols[p * 16 + 2 * s + member] * B, B)
                ref[:, pl.ds(col, B)] += values[3 * s + 1 + member]

    grad_ref[...] = (first_ref[...] + second_ref[...]).astype(jnp.bfloat16)


def place(block_cols, block_rows, back):
    return pl.pallas_call(
        place_kernel,
        out_shape=[jax.ShapeDtypeStruct((S, 128 * B), jnp.bfloat16)] * 2 + [pltpu.VMEM((S, 128), jnp.float32)],
        in_specs=[SMEM, SMEM] + vmem(1),
        scratch_shapes=[pltpu.VMEM((S, 128 * B), jnp.float32)] * 2,
        compiler_params=ROOM,
        name="place",
    )(block_cols, block_rows, *here(back))


def shards(shots_in, cotangent, blocks, block_rows, block_cols):
    core = position()[0]
    permute = functools.partial(lax.ppermute, axis_name=AXES)
    exchange = functools.partial(
        lax.all_to_all, axis_name=AXES, split_axis=0, concat_axis=0, axis_index_groups=groups(), tiled=True
    )

    received = exchange(gather(block_cols, block_rows, shots_in, cotangent)).reshape(OWNERS * S, MESSAGE)
    theirs = lax.dynamic_slice_in_dim(received, (1 - core) * HALF, HALF, axis=1)
    other = permute(theirs, perm=moves(lambda a, b, c: (a, b, 1 - c)))
    result = apply(received, blocks)
    send, keep = grad(received, other, result)
    got = permute(send, perm=moves(lambda a, b, c: (a, b ^ 1, c)))
    back = exchange(result.reshape(OWNERS, S, MESSAGE + SCALES))
    *parts, own = pairs(keep, got)
    parts = [
        permute(part, perm=moves(lambda a, b, c, d=d: (a, (b + 2 * d) % Y, c))) for d, part in zip(PAIR_STEPS, parts)
    ]
    *parts, own = cut(own, parts)
    parts = [
        permute(part, perm=moves(lambda a, b, c, d=d: (a ^ (d + 1), b, c))) for d, part in enumerate(parts)
    ]
    shots_out, input_grad, placed = place(block_cols, block_rows, back)
    mine, send = last(own, parts, placed)
    swapped = permute(send, perm=moves(lambda a, b, c: (a, b, 1 - c)))
    weight_grad = jnp.where(core == 0, jnp.concatenate([mine, swapped]), jnp.concatenate([swapped, mine]))
    return shots_out, input_grad, weight_grad


def solution(mesh):
    return jax.shard_map(
        shards,
        mesh=mesh,
        in_specs=(P(AXES, None), P(AXES, None), P("fsdp", None, None), P(), P()),
        out_specs=(P(AXES, None), P(AXES, None), P("fsdp", "dp", None)),
        check_vma=False,
    )
```

```python
import functools

import jax
import jax.numpy as jnp
from jax import lax
from jax.experimental import pallas as pl
from jax.experimental.pallas import tpu as pltpu
from jax.sharding import PartitionSpec as P

AXES = ("dp", "fsdp")
XL, Y, CORES, XH, Z = 4, 8, 2, 2, 8
OWNERS = XH * Z
S = 8
B = 256
HALF = 12 * B
MESSAGE = 2 * HALF
SCALES = 128
STEPS = 16.0
PAIR_STEPS = (1, 3, 2)
SMEM = pl.BlockSpec(memory_space=pltpu.SMEM)
ANY = pl.BlockSpec(memory_space=pl.ANY)
ROOM = pltpu.CompilerParams(vmem_limit_bytes=24 * 2**20)


def device(xl, y, core, xh, z):
    return (((xl * Y + y) * CORES + core) * XH + xh) * Z + z


def position():
    dp = lax.axis_index("dp")
    return lax.rem(dp, CORES), lax.rem(lax.div(dp, CORES), Y), lax.div(dp, CORES * Y)


def groups():
    return [
        [device((xl + 2 * xh) % XL, y, core, xh, z) for xh in range(XH) for z in range(Z)]
        for xl in range(XL)
        for y in range(Y)
        for core in range(CORES)
    ]


def moves(target):
    return [
        (device(xl, y, core, xh, z), device(*target(xl, y, core), xh, z))
        for xl in range(XL)
        for y in range(Y)
        for core in range(CORES)
        for xh in range(XH)
        for z in range(Z)
    ]


LONG = pl.CostEstimate(flops=80_000_000_000, bytes_accessed=1_000_000, transcendentals=0)


def gather_kernel(cols, rows, x_hbm, g_hbm, out_hbm, x_ref, g_ref, out_ref, in_sems, out_sems):
    loads = [
        pltpu.make_async_copy(x_hbm, x_ref, in_sems.at[0]),
        pltpu.make_async_copy(g_hbm, g_ref, in_sems.at[1]),
    ]
    for load in loads:
        load.start()
    for load in loads:
        load.wait()
    stores = []
    for chunk in range(4):
        owners = slice(chunk * 4, chunk * 4 + 4)
        for p in range(owners.start, owners.stop):
            for half in range(2):
                first = p * 16 + half * 8
                for j in range(8):
                    col = pl.multiple_of(cols[first + j] * B, B)
                    out_ref[p, :, at(half * 12 + j)] = x_ref[:, pl.ds(col, B)]
                for j in range(4):
                    row = pl.multiple_of(rows[first + 2 * j] * B, B)
                    out_ref[p, :, at(half * 12 + 8 + j)] = g_ref[:, pl.ds(row, B)]
        stores.append(pltpu.make_async_copy(out_ref.at[owners], out_hbm.at[owners], out_sems.at[chunk]))
        stores[-1].start()
    for store in stores:
        store.wait()


def gather(block_cols, block_rows, shots_in, cotangent):
    message = (OWNERS, S, MESSAGE)
    return pl.pallas_call(
        gather_kernel,
        out_shape=jax.ShapeDtypeStruct(message, jnp.bfloat16),
        in_specs=[SMEM, SMEM, ANY, ANY],
        out_specs=ANY,
        scratch_shapes=[pltpu.VMEM((S, 128 * B), jnp.bfloat16)] * 2
        + [
            pltpu.VMEM(message, jnp.bfloat16),
            pltpu.SemaphoreType.DMA((2,)),
            pltpu.SemaphoreType.DMA((4,)),
        ],
        name="gather",
    )(block_cols, block_rows, shots_in, cotangent)


def fixed(v):
    top = jnp.max(jnp.abs(v), axis=1, keepdims=True)
    e = jnp.ceil(jnp.log2(jnp.maximum(top, 2.0**-120)) * STEPS + 0.01)
    return jnp.round(v * (jnp.exp2(e * (-1.0 / STEPS)) * 32760.0)).astype(jnp.int32).astype(jnp.int16), e


def decoded(e):
    return jnp.exp2(e.astype(jnp.int32).astype(jnp.float32) * (1.0 / STEPS)) * (1.0 / 32760.0)


def widened(q):
    return q.astype(jnp.int32).astype(jnp.float32)


def at(j, width=B):
    return slice(j * B, j * B + width)


def dot(u, v, over):
    return lax.dot_general(u, v, (over, ((), ())), preferred_element_type=jnp.float32)


def put_scales(ref, scales):
    lanes = lax.broadcasted_iota(jnp.int32, (scales[0].shape[0], SCALES), 1)
    out = jnp.zeros(lanes.shape, jnp.float32)
    for j, e in enumerate(scales):
        out = jnp.where(lanes == j, e, out)
    ref[:, ref.shape[1] - SCALES :] = out.astype(jnp.int32).astype(jnp.int16)


def grad_kernel(in_ref, other_ref, after_ref, first_ref, second_ref, keep_ref, wg_ref):
    core, y, _ = position()
    parity = y % 2
    scales = []
    for j in range(8):
        own = lambda slot: in_ref[:, pl.ds(pl.multiple_of(core * HALF + slot * B, B), B)]
        x0, g0 = own(j), own(8 + j // 2)
        x1, g1 = other_ref[:, at(j)], other_ref[:, at(8 + j // 2)]
        wg = dot(x0, g0, ((0,), (0,))) + dot(x1, g1, ((0,), (0,)))
        wg_ref[...] = wg.reshape(16, 2, S, B)
        keep_ref[:, at(j)] = wg_ref[:, pl.ds(parity, 1)].reshape(128, B)
        q, e = fixed(wg_ref[:, pl.ds(1 - parity, 1)].reshape(128, B))
        (first_ref, second_ref)[j // 4][:, at(j % 4)] = q
        scales.append(e)
    put_scales(first_ref, scales[:4])
    put_scales(second_ref, scales[4:])


def apply_kernel(in_ref, w_ref, out_ref):
    scales = []
    for s in range(8):
        first = s // 4 * 12 + s % 4 * 2
        x0, x1, g = in_ref[:, at(first)], in_ref[:, at(first + 1)], in_ref[:, at(s // 4 * 12 + 8 + s % 4)]
        w0, w1 = w_ref[2 * s], w_ref[2 * s + 1]
        values = (
            dot(x0, w0, ((1,), (0,))) + dot(x1, w1, ((1,), (0,))),
            dot(g, w0, ((1,), (1,))),
            dot(g, w1, ((1,), (1,))),
        )
        for slot, value in enumerate(values):
            q, e = fixed(value)
            out_ref[:, at(3 * s + slot)] = q
            scales.append(e)
    put_scales(out_ref, scales)


def here(*arrays):
    return [pltpu.with_memory_space_constraint(a, pltpu.VMEM) for a in arrays]


def vmem(n):
    return [pl.BlockSpec(memory_space=pltpu.VMEM)] * n


PART = 8 * B + SCALES


def grad(received, other, after):
    return pl.pallas_call(
        grad_kernel,
        out_shape=[pltpu.VMEM((128, 4 * B + SCALES), jnp.int16)] * 2 + [pltpu.VMEM((128, 8 * B), jnp.float32)],
        in_specs=vmem(2) + [ANY],
        out_specs=vmem(3),
        scratch_shapes=[pltpu.VMEM((16, 2, S, B), jnp.float32)],
        compiler_params=ROOM,
        name="grad",
    )(*here(received, other), after)


def half_kernel(in_ref, out_ref):
    theirs = 1 - position()[0]
    for j in range(12):
        out_ref[:, at(j)] = in_ref[:, pl.ds(pl.multiple_of(theirs * HALF + j * B, B), B)]


def half(received):
    return pl.pallas_call(
        half_kernel,
        out_shape=pltpu.VMEM((OWNERS * S, HALF), jnp.bfloat16),
        in_specs=vmem(1),
        out_specs=vmem(1)[0],
        compiler_params=ROOM,
        name="half",
    )(*here(received))


def apply(received, blocks):
    return pl.pallas_call(
        apply_kernel,
        out_shape=jax.ShapeDtypeStruct((OWNERS * S, MESSAGE + SCALES), jnp.int16),
        in_specs=vmem(2),
        compiler_params=ROOM,
        cost_estimate=pl.CostEstimate(flops=5_000_000_000, bytes_accessed=20_000_000, transcendentals=0),
        name="apply",
    )(*here(received, blocks))


def pairs_kernel(keep_ref, first_ref, second_ref, *refs):
    outs, own_ref, total_ref = refs[:3], refs[3], refs[4]
    pair = position()[1] // 2
    got = (first_ref, second_ref)
    before = [decoded(ref[:, 4 * B :]) for ref in got]
    scales = [[] for _ in range(3)]
    for j in range(8):
        i = j % 4
        total = keep_ref[:, at(j)] + widened(got[j // 4][:, at(i)]) * before[j // 4][:, i : i + 1]
        total_ref[...] = total.reshape(XL, 4, S, B)
        own_ref[:, at(j)] = total_ref[:, pl.ds(pair, 1)].reshape(32, B)
        for d in range(3):
            q, e = fixed(total_ref[:, pl.ds(lax.rem(pair + PAIR_STEPS[d], 4), 1)].reshape(32, B))
            outs[d][:, at(j)] = q
            scales[d].append(e)
    for d in range(3):
        put_scales(outs[d], scales[d])


def pairs(keep, first, second):
    return pl.pallas_call(
        pairs_kernel,
        out_shape=[pltpu.VMEM((32, PART), jnp.int16)] * 3
        + [pltpu.VMEM((32, 8 * B), jnp.float32)],
        in_specs=vmem(3),
        out_specs=vmem(4),
        scratch_shapes=[pltpu.VMEM((XL, 4, S, B), jnp.float32)],
        compiler_params=ROOM,
        cost_estimate=LONG,
        name="pairs",
    )(*here(keep, first, second))


def cut_kernel(own_ref, a_ref, b_ref, c_ref, *refs):
    outs, keep_ref, total_ref = refs[:3], refs[3], refs[4]
    xl = position()[2]
    ins = (a_ref, b_ref, c_ref)
    before = [decoded(ref[:, 8 * B :]) for ref in ins]
    scales = [[] for _ in range(3)]
    for j in range(8):
        total = own_ref[:, at(j)]
        for ref, scale in zip(ins, before):
            total = total + widened(ref[:, at(j)]) * scale[:, j : j + 1]
        total_ref[...] = total.reshape(XL, S, B)
        keep_ref[:, at(j)] = total_ref[xl]
        for d in range(3):
            q, e = fixed(total_ref[xl ^ (d + 1)])
            outs[d][:, at(j)] = q
            scales[d].append(e)
    for d in range(3):
        put_scales(outs[d], scales[d])


def cut(own, parts):
    return pl.pallas_call(
        cut_kernel,
        out_shape=[pltpu.VMEM((S, PART), jnp.int16)] * 3 + [pltpu.VMEM((S, 8 * B), jnp.float32)],
        in_specs=vmem(4),
        out_specs=vmem(4),
        scratch_shapes=[pltpu.VMEM((XL, S, B), jnp.float32)],
        compiler_params=ROOM,
        name="cut",
    )(*here(own, *parts))


def last_kernel(own_ref, a_ref, b_ref, c_ref, mine_ref, send_ref):
    ins = (a_ref, b_ref, c_ref)
    scales = [decoded(ref[:, 8 * B :]) for ref in ins]
    first = position()[0] == 0
    for j in range(8):
        total = own_ref[:, at(j)]
        for ref, scale in zip(ins, scales):
            total = total + widened(ref[:, at(j)]) * scale[:, j : j + 1]
        total = total * 8192.0**-0.5
        top, bottom = total[:4], total[4:]
        mine_ref[j] = jnp.where(first, top, bottom)
        send_ref[j] = jnp.where(first, bottom, top)


def last(own, parts):
    return pl.pallas_call(
        last_kernel,
        out_shape=[pltpu.VMEM((8, 4, B), jnp.float32)] * 2,
        in_specs=vmem(4),
        out_specs=vmem(2),
        compiler_params=ROOM,
        name="last",
    )(*here(own, *parts))


def place_kernel(cols, rows, in_ref, out_ref, grad_ref, first_ref, second_ref):
    totals = (first_ref, second_ref)
    for ref in totals:
        ref[...] = jnp.zeros_like(ref)

    @pl.loop(0, OWNERS)
    def _(p):
        scale = decoded(in_ref[p, :, MESSAGE:])
        values = [widened(in_ref[p, :, at(j)]) * scale[:, j : j + 1] for j in range(24)]
        for s in range(8):
            row = pl.multiple_of(rows[p * 16 + 2 * s] * B, B)
            out_ref[:, pl.ds(row, B)] = values[3 * s].astype(jnp.bfloat16)
            for member, ref in enumerate(totals):
                col = pl.multiple_of(cols[p * 16 + 2 * s + member] * B, B)
                ref[:, pl.ds(col, B)] += values[3 * s + 1 + member]

    grad_ref[...] = (first_ref[...] + second_ref[...]).astype(jnp.bfloat16)


def place(block_cols, block_rows, back):
    return pl.pallas_call(
        place_kernel,
        out_shape=[jax.ShapeDtypeStruct((S, 128 * B), jnp.bfloat16)] * 2,
        in_specs=[SMEM, SMEM] + vmem(1),
        scratch_shapes=[pltpu.VMEM((S, 128 * B), jnp.float32)] * 2,
        compiler_params=ROOM,
        name="place",
    )(block_cols, block_rows, *here(back))


def shards(shots_in, cotangent, blocks, block_rows, block_cols):
    core = position()[0]
    permute = functools.partial(lax.ppermute, axis_name=AXES)
    exchange = functools.partial(
        lax.all_to_all, axis_name=AXES, split_axis=0, concat_axis=0, axis_index_groups=groups(), tiled=True
    )

    received = exchange(gather(block_cols, block_rows, shots_in, cotangent)).reshape(OWNERS * S, MESSAGE)
    other = permute(half(received), perm=moves(lambda a, b, c: (a, b, 1 - c)))
    result = apply(received, blocks)
    first, second, keep = grad(received, other, result)
    first = permute(first, perm=moves(lambda a, b, c: (a, b ^ 1, c)))
    second = permute(second, perm=moves(lambda a, b, c: (a, ((b + 1) ^ 1) - 1 & 7, c)))
    back = exchange(result.reshape(OWNERS, S, MESSAGE + SCALES))
    *parts, own = pairs(keep, first, second)
    parts = [
        permute(part, perm=moves(lambda a, b, c, d=d: (a, (b + 2 * d) % Y, c))) for d, part in zip(PAIR_STEPS, parts)
    ]
    *parts, own = cut(own, parts)
    parts = [
        permute(part, perm=moves(lambda a, b, c, d=d: (a ^ (d + 1), b, c))) for d, part in enumerate(parts)
    ]
    mine, send = last(own, parts)
    swapped = permute(send, perm=moves(lambda a, b, c: (a, b, 1 - c)))
    weight_grad = jnp.where(core == 0, jnp.concatenate([mine, swapped]), jnp.concatenate([swapped, mine]))
    shots_out, input_grad = place(block_cols, block_rows, back)
    return shots_out, input_grad, weight_grad


def solution(mesh):
    return jax.shard_map(
        shards,
        mesh=mesh,
        in_specs=(P(AXES, None), P(AXES, None), P("fsdp", None, None), P(), P()),
        out_specs=(P(AXES, None), P(AXES, None), P("fsdp", "dp", None)),
        check_vma=False,
    )
```

```python
import functools

import jax
import jax.numpy as jnp
from jax import lax
from jax.experimental import pallas as pl
from jax.experimental.pallas import tpu as pltpu
from jax.sharding import PartitionSpec as P

AXES = ("dp", "fsdp")
XL, Y, CORES, XH, Z = 4, 8, 2, 2, 8
OWNERS = XH * Z
S = 8
B = 256
HALF = 12 * B
MESSAGE = 2 * HALF
SCALES = 128
STEPS = 16.0
PAIR_STEPS = (1, 3, 2)
SMEM = pl.BlockSpec(memory_space=pltpu.SMEM)
ANY = pl.BlockSpec(memory_space=pl.ANY)
ROOM = pltpu.CompilerParams(vmem_limit_bytes=24 * 2**20)


def device(xl, y, core, xh, z):
    return (((xl * Y + y) * CORES + core) * XH + xh) * Z + z


def position():
    dp = lax.axis_index("dp")
    return lax.rem(dp, CORES), lax.rem(lax.div(dp, CORES), Y), lax.div(dp, CORES * Y)


def groups():
    return [
        [device((xl + 2 * xh) % XL, y, core, xh, z) for xh in range(XH) for z in range(Z)]
        for xl in range(XL)
        for y in range(Y)
        for core in range(CORES)
    ]


def moves(target):
    return [
        (device(xl, y, core, xh, z), device(*target(xl, y, core), xh, z))
        for xl in range(XL)
        for y in range(Y)
        for core in range(CORES)
        for xh in range(XH)
        for z in range(Z)
    ]


LONG = pl.CostEstimate(flops=80_000_000_000, bytes_accessed=1_000_000, transcendentals=0)


def gather_kernel(cols, rows, x_hbm, g_hbm, out_hbm, x_ref, g_ref, out_ref, in_sems, out_sems):
    loads = [
        pltpu.make_async_copy(x_hbm, x_ref, in_sems.at[0]),
        pltpu.make_async_copy(g_hbm, g_ref, in_sems.at[1]),
    ]
    for load in loads:
        load.start()
    for load in loads:
        load.wait()
    stores = []
    for chunk in range(4):
        owners = slice(chunk * 4, chunk * 4 + 4)
        for p in range(owners.start, owners.stop):
            for half in range(2):
                first = p * 16 + half * 8
                for j in range(8):
                    col = pl.multiple_of(cols[first + j] * B, B)
                    out_ref[p, :, at(half * 12 + j)] = x_ref[:, pl.ds(col, B)]
                for j in range(4):
                    row = pl.multiple_of(rows[first + 2 * j] * B, B)
                    out_ref[p, :, at(half * 12 + 8 + j)] = g_ref[:, pl.ds(row, B)]
        stores.append(pltpu.make_async_copy(out_ref.at[owners], out_hbm.at[owners], out_sems.at[chunk]))
        stores[-1].start()
    for store in stores:
        store.wait()


def gather(block_cols, block_rows, shots_in, cotangent):
    message = (OWNERS, S, MESSAGE)
    return pl.pallas_call(
        gather_kernel,
        out_shape=jax.ShapeDtypeStruct(message, jnp.bfloat16),
        in_specs=[SMEM, SMEM, ANY, ANY],
        out_specs=ANY,
        scratch_shapes=[pltpu.VMEM((S, 128 * B), jnp.bfloat16)] * 2
        + [
            pltpu.VMEM(message, jnp.bfloat16),
            pltpu.SemaphoreType.DMA((2,)),
            pltpu.SemaphoreType.DMA((4,)),
        ],
        name="gather",
    )(block_cols, block_rows, shots_in, cotangent)


def fixed(v):
    top = jnp.max(jnp.abs(v), axis=1, keepdims=True)
    e = jnp.ceil(jnp.log2(jnp.maximum(top, 2.0**-120)) * STEPS + 0.01)
    return jnp.round(v * (jnp.exp2(e * (-1.0 / STEPS)) * 32760.0)).astype(jnp.int32).astype(jnp.int16), e


def decoded(e):
    return jnp.exp2(e.astype(jnp.int32).astype(jnp.float32) * (1.0 / STEPS)) * (1.0 / 32760.0)


def widened(q):
    return q.astype(jnp.int32).astype(jnp.float32)


def at(j, width=B):
    return slice(j * B, j * B + width)


def dot(u, v, over):
    return lax.dot_general(u, v, (over, ((), ())), preferred_element_type=jnp.float32)


def put_scales(ref, scales):
    lanes = lax.broadcasted_iota(jnp.int32, (scales[0].shape[0], SCALES), 1)
    out = jnp.zeros(lanes.shape, jnp.float32)
    for j, e in enumerate(scales):
        out = jnp.where(lanes == j, e, out)
    ref[:, ref.shape[1] - SCALES :] = out.astype(jnp.int32).astype(jnp.int16)


def grad_kernel(in_ref, other_ref, after_ref, first_ref, second_ref, keep_ref, wg_ref):
    core, y, _ = position()
    parity = y % 2
    scales = []
    for j in range(8):
        own = lambda slot: in_ref[:, pl.ds(pl.multiple_of(core * HALF + slot * B, B), B)]
        x0, g0 = own(j), own(8 + j // 2)
        x1, g1 = other_ref[:, at(j)], other_ref[:, at(8 + j // 2)]
        wg = dot(x0, g0, ((0,), (0,))) + dot(x1, g1, ((0,), (0,)))
        wg_ref[...] = wg.reshape(16, 2, S, B)
        keep_ref[:, at(j)] = wg_ref[:, pl.ds(parity, 1)].reshape(128, B)
        q, e = fixed(wg_ref[:, pl.ds(1 - parity, 1)].reshape(128, B))
        (first_ref, second_ref)[j // 4][:, at(j % 4)] = q
        scales.append(e)
    put_scales(first_ref, scales[:4])
    put_scales(second_ref, scales[4:])


def apply_kernel(in_ref, w_ref, out_ref):
    scales = []
    for s in range(8):
        first = s // 4 * 12 + s % 4 * 2
        x0, x1, g = in_ref[:, at(first)], in_ref[:, at(first + 1)], in_ref[:, at(s // 4 * 12 + 8 + s % 4)]
        w0, w1 = w_ref[2 * s], w_ref[2 * s + 1]
        values = (
            dot(x0, w0, ((1,), (0,))) + dot(x1, w1, ((1,), (0,))),
            dot(g, w0, ((1,), (1,))),
            dot(g, w1, ((1,), (1,))),
        )
        for slot, value in enumerate(values):
            q, e = fixed(value)
            out_ref[:, at(3 * s + slot)] = q
            scales.append(e)
    put_scales(out_ref, scales)


def here(*arrays):
    return [pltpu.with_memory_space_constraint(a, pltpu.VMEM) for a in arrays]


def vmem(n):
    return [pl.BlockSpec(memory_space=pltpu.VMEM)] * n


PART = 8 * B + SCALES


def grad(received, other, after):
    return pl.pallas_call(
        grad_kernel,
        out_shape=[pltpu.VMEM((128, 4 * B + SCALES), jnp.int16)] * 2 + [pltpu.VMEM((128, 8 * B), jnp.float32)],
        in_specs=vmem(2) + [ANY],
        out_specs=vmem(3),
        scratch_shapes=[pltpu.VMEM((16, 2, S, B), jnp.float32)],
        compiler_params=ROOM,
        name="grad",
    )(*here(received, other), after)


def half_kernel(in_ref, out_ref):
    theirs = 1 - position()[0]
    for j in range(12):
        out_ref[:, at(j)] = in_ref[:, pl.ds(pl.multiple_of(theirs * HALF + j * B, B), B)]


def half(received):
    return pl.pallas_call(
        half_kernel,
        out_shape=pltpu.VMEM((OWNERS * S, HALF), jnp.bfloat16),
        in_specs=vmem(1),
        out_specs=vmem(1)[0],
        compiler_params=ROOM,
        name="half",
    )(*here(received))


def apply(received, blocks):
    return pl.pallas_call(
        apply_kernel,
        out_shape=jax.ShapeDtypeStruct((OWNERS * S, MESSAGE + SCALES), jnp.int16),
        in_specs=vmem(2),
        compiler_params=ROOM,
        cost_estimate=pl.CostEstimate(flops=5_000_000_000, bytes_accessed=20_000_000, transcendentals=0),
        name="apply",
    )(*here(received, blocks))


def pairs_kernel(keep_ref, first_ref, second_ref, *refs):
    outs, own_ref, total_ref = refs[:3], refs[3], refs[4]
    pair = position()[1] // 2
    got = (first_ref, second_ref)
    before = [decoded(ref[:, 4 * B :]) for ref in got]
    scales = [[] for _ in range(3)]
    for j in range(8):
        i = j % 4
        total = keep_ref[:, at(j)] + widened(got[j // 4][:, at(i)]) * before[j // 4][:, i : i + 1]
        total_ref[...] = total.reshape(XL, 4, S, B)
        own_ref[:, at(j)] = total_ref[:, pl.ds(pair, 1)].reshape(32, B)
        for d in range(3):
            q, e = fixed(total_ref[:, pl.ds(lax.rem(pair + PAIR_STEPS[d], 4), 1)].reshape(32, B))
            outs[d][:, at(j)] = q
            scales[d].append(e)
    for d in range(3):
        put_scales(outs[d], scales[d])


def pairs(keep, first, second):
    return pl.pallas_call(
        pairs_kernel,
        out_shape=[pltpu.VMEM((32, PART), jnp.int16)] * 3
        + [pltpu.VMEM((32, 8 * B), jnp.float32)],
        in_specs=vmem(3),
        out_specs=vmem(4),
        scratch_shapes=[pltpu.VMEM((XL, 4, S, B), jnp.float32)],
        compiler_params=ROOM,
        cost_estimate=LONG,
        name="pairs",
    )(*here(keep, first, second))


def cut_kernel(own_ref, a_ref, b_ref, c_ref, *refs):
    outs, keep_ref, total_ref = refs[:3], refs[3], refs[4]
    xl = position()[2]
    ins = (a_ref, b_ref, c_ref)
    before = [decoded(ref[:, 8 * B :]) for ref in ins]
    scales = [[] for _ in range(3)]
    for j in range(8):
        total = own_ref[:, at(j)]
        for ref, scale in zip(ins, before):
            total = total + widened(ref[:, at(j)]) * scale[:, j : j + 1]
        total_ref[...] = total.reshape(XL, S, B)
        keep_ref[:, at(j)] = total_ref[xl]
        for d in range(3):
            q, e = fixed(total_ref[xl ^ (d + 1)])
            outs[d][:, at(j)] = q
            scales[d].append(e)
    for d in range(3):
        put_scales(outs[d], scales[d])


def cut(own, parts):
    return pl.pallas_call(
        cut_kernel,
        out_shape=[pltpu.VMEM((S, PART), jnp.int16)] * 3 + [pltpu.VMEM((S, 8 * B), jnp.float32)],
        in_specs=vmem(4),
        out_specs=vmem(4),
        scratch_shapes=[pltpu.VMEM((XL, S, B), jnp.float32)],
        compiler_params=ROOM,
        name="cut",
    )(*here(own, *parts))


def last_kernel(own_ref, a_ref, b_ref, c_ref, mine_ref, send_ref):
    ins = (a_ref, b_ref, c_ref)
    scales = [decoded(ref[:, 8 * B :]) for ref in ins]
    first = position()[0] == 0
    for j in range(8):
        total = own_ref[:, at(j)]
        for ref, scale in zip(ins, scales):
            total = total + widened(ref[:, at(j)]) * scale[:, j : j + 1]
        total = total * 8192.0**-0.5
        top, bottom = total[:4], total[4:]
        mine_ref[j] = jnp.where(first, top, bottom)
        send_ref[j] = jnp.where(first, bottom, top)


def last(own, parts):
    return pl.pallas_call(
        last_kernel,
        out_shape=[pltpu.VMEM((8, 4, B), jnp.float32)] * 2,
        in_specs=vmem(4),
        out_specs=vmem(2),
        compiler_params=ROOM,
        name="last",
    )(*here(own, *parts))


def place_kernel(cols, rows, in_ref, out_ref, grad_ref, mark_ref, first_ref, second_ref):
    mark_ref[...] = jnp.zeros_like(mark_ref)
    totals = (first_ref, second_ref)
    for ref in totals:
        ref[...] = jnp.zeros_like(ref)

    @pl.loop(0, OWNERS, unroll=8)
    def _(p):
        scale = decoded(in_ref[p, :, MESSAGE:])
        values = [widened(in_ref[p, :, at(j)]) * scale[:, j : j + 1] for j in range(24)]
        for s in range(8):
            row = pl.multiple_of(rows[p * 16 + 2 * s] * B, B)
            out_ref[:, pl.ds(row, B)] = values[3 * s].astype(jnp.bfloat16)
            for member, ref in enumerate(totals):
                col = pl.multiple_of(cols[p * 16 + 2 * s + member] * B, B)
                ref[:, pl.ds(col, B)] += values[3 * s + 1 + member]

    grad_ref[...] = (first_ref[...] + second_ref[...]).astype(jnp.bfloat16)


def place(block_cols, block_rows, back):
    return pl.pallas_call(
        place_kernel,
        out_shape=[jax.ShapeDtypeStruct((S, 128 * B), jnp.bfloat16)] * 2 + [pltpu.VMEM((S, 128), jnp.float32)],
        in_specs=[SMEM, SMEM] + vmem(1),
        scratch_shapes=[pltpu.VMEM((S, 128 * B), jnp.float32)] * 2,
        compiler_params=ROOM,
        name="place",
    )(block_cols, block_rows, *here(back))


def join_kernel(mine_ref, swapped_ref, after_ref, out_ref):
    first = position()[0] == 0
    mine, swapped = mine_ref[...], swapped_ref[...]
    out_ref[:8] = jnp.where(first, mine, swapped)
    out_ref[8:] = jnp.where(first, swapped, mine)


def join(mine, swapped, after):
    return pl.pallas_call(
        join_kernel,
        out_shape=jax.ShapeDtypeStruct((16, 4, B), jnp.float32),
        in_specs=vmem(3),
        compiler_params=ROOM,
        name="join",
    )(*here(mine, swapped, after))


def shards(shots_in, cotangent, blocks, block_rows, block_cols):
    permute = functools.partial(lax.ppermute, axis_name=AXES)
    exchange = functools.partial(
        lax.all_to_all, axis_name=AXES, split_axis=0, concat_axis=0, axis_index_groups=groups(), tiled=True
    )

    received = exchange(gather(block_cols, block_rows, shots_in, cotangent)).reshape(OWNERS * S, MESSAGE)
    other = permute(half(received), perm=moves(lambda a, b, c: (a, b, 1 - c)))
    result = apply(received, blocks)
    first, second, keep = grad(received, other, result)
    first = permute(first, perm=moves(lambda a, b, c: (a, b ^ 1, c)))
    second = permute(second, perm=moves(lambda a, b, c: (a, ((b + 1) ^ 1) - 1 & 7, c)))
    back = exchange(result.reshape(OWNERS, S, MESSAGE + SCALES))
    *parts, own = pairs(keep, first, second)
    parts = [
        permute(part, perm=moves(lambda a, b, c, d=d: (a, (b + 2 * d) % Y, c))) for d, part in zip(PAIR_STEPS, parts)
    ]
    *parts, own = cut(own, parts)
    parts = [
        permute(part, perm=moves(lambda a, b, c, d=d: (a ^ (d + 1), b, c))) for d, part in enumerate(parts)
    ]
    mine, send = last(own, parts)
    swapped = permute(send, perm=moves(lambda a, b, c: (a, b, 1 - c)))
    shots_out, input_grad, placed = place(block_cols, block_rows, back)
    weight_grad = join(mine, swapped, placed)
    return shots_out, input_grad, weight_grad


def solution(mesh):
    return jax.shard_map(
        shards,
        mesh=mesh,
        in_specs=(P(AXES, None), P(AXES, None), P("fsdp", None, None), P(), P()),
        out_specs=(P(AXES, None), P(AXES, None), P("fsdp", "dp", None)),
        check_vma=False,
    )
```

```python
import functools

import jax
import jax.numpy as jnp
from jax import lax
from jax.experimental import pallas as pl
from jax.experimental.pallas import tpu as pltpu
from jax.sharding import PartitionSpec as P

AXES = ("dp", "fsdp")
XL, Y, CORES, XH, Z = 4, 8, 2, 2, 8
OWNERS = XH * Z
S = 8
B = 256
HALF = 12 * B
MESSAGE = 2 * HALF
SCALES = 128
STEPS = 16.0
PAIR_STEPS = (2, 1, 3)
SMEM = pl.BlockSpec(memory_space=pltpu.SMEM)
ANY = pl.BlockSpec(memory_space=pl.ANY)
ROOM = pltpu.CompilerParams(vmem_limit_bytes=24 * 2**20)


def device(xl, y, core, xh, z):
    return (((xl * Y + y) * CORES + core) * XH + xh) * Z + z


def position():
    dp = lax.axis_index("dp")
    return lax.rem(dp, CORES), lax.rem(lax.div(dp, CORES), Y), lax.div(dp, CORES * Y)


def groups():
    return [
        [device((xl + 2 * xh) % XL, y, core, xh, z) for xh in range(XH) for z in range(Z)]
        for xl in range(XL)
        for y in range(Y)
        for core in range(CORES)
    ]


def moves(target):
    return [
        (device(xl, y, core, xh, z), device(*target(xl, y, core), xh, z))
        for xl in range(XL)
        for y in range(Y)
        for core in range(CORES)
        for xh in range(XH)
        for z in range(Z)
    ]


LONG = pl.CostEstimate(flops=80_000_000_000, bytes_accessed=1_000_000, transcendentals=0)


def gather_kernel(cols, rows, x_hbm, g_hbm, out_hbm, x_ref, g_ref, out_ref, in_sems, out_sems):
    loads = [
        pltpu.make_async_copy(x_hbm, x_ref, in_sems.at[0]),
        pltpu.make_async_copy(g_hbm, g_ref, in_sems.at[1]),
    ]
    for load in loads:
        load.start()
    for load in loads:
        load.wait()
    stores = []
    for chunk in range(4):
        owners = slice(chunk * 4, chunk * 4 + 4)
        for p in range(owners.start, owners.stop):
            for half in range(2):
                first = p * 16 + half * 8
                for j in range(8):
                    col = pl.multiple_of(cols[first + j] * B, B)
                    out_ref[p, :, at(half * 12 + j)] = x_ref[:, pl.ds(col, B)]
                for j in range(4):
                    row = pl.multiple_of(rows[first + 2 * j] * B, B)
                    out_ref[p, :, at(half * 12 + 8 + j)] = g_ref[:, pl.ds(row, B)]
        stores.append(pltpu.make_async_copy(out_ref.at[owners], out_hbm.at[owners], out_sems.at[chunk]))
        stores[-1].start()
    for store in stores:
        store.wait()


def gather(block_cols, block_rows, shots_in, cotangent):
    message = (OWNERS, S, MESSAGE)
    return pl.pallas_call(
        gather_kernel,
        out_shape=jax.ShapeDtypeStruct(message, jnp.bfloat16),
        in_specs=[SMEM, SMEM, ANY, ANY],
        out_specs=ANY,
        scratch_shapes=[pltpu.VMEM((S, 128 * B), jnp.bfloat16)] * 2
        + [
            pltpu.VMEM(message, jnp.bfloat16),
            pltpu.SemaphoreType.DMA((2,)),
            pltpu.SemaphoreType.DMA((4,)),
        ],
        name="gather",
    )(block_cols, block_rows, shots_in, cotangent)


def fixed(v):
    top = jnp.max(jnp.abs(v), axis=1, keepdims=True)
    e = jnp.ceil(jnp.log2(jnp.maximum(top, 2.0**-120)) * STEPS + 0.01)
    return jnp.round(v * (jnp.exp2(e * (-1.0 / STEPS)) * 32760.0)).astype(jnp.int32).astype(jnp.int16), e


def decoded(e):
    return jnp.exp2(e.astype(jnp.int32).astype(jnp.float32) * (1.0 / STEPS)) * (1.0 / 32760.0)


def widened(q):
    return q.astype(jnp.int32).astype(jnp.float32)


def at(j, width=B):
    return slice(j * B, j * B + width)


def dot(u, v, over):
    return lax.dot_general(u, v, (over, ((), ())), preferred_element_type=jnp.float32)


def put_scales(ref, scales):
    lanes = lax.broadcasted_iota(jnp.int32, (scales[0].shape[0], SCALES), 1)
    out = jnp.zeros(lanes.shape, jnp.float32)
    for j, e in enumerate(scales):
        out = jnp.where(lanes == j, e, out)
    ref[:, ref.shape[1] - SCALES :] = out.astype(jnp.int32).astype(jnp.int16)


def grad_kernel(in_ref, other_ref, after_ref, first_ref, second_ref, keep_ref, wg_ref):
    core, y, _ = position()
    parity = y % 2
    scales = []
    for j in range(8):
        own = lambda slot: in_ref[:, pl.ds(pl.multiple_of(core * HALF + slot * B, B), B)]
        x0, g0 = own(j), own(8 + j // 2)
        x1, g1 = other_ref[:, at(j)], other_ref[:, at(8 + j // 2)]
        wg = dot(x0, g0, ((0,), (0,))) + dot(x1, g1, ((0,), (0,)))
        wg_ref[...] = wg.reshape(16, 2, S, B)
        keep_ref[:, at(j)] = wg_ref[:, pl.ds(parity, 1)].reshape(128, B)
        q, e = fixed(wg_ref[:, pl.ds(1 - parity, 1)].reshape(128, B))
        (first_ref, second_ref)[j // 4][:, at(j % 4)] = q
        scales.append(e)
    put_scales(first_ref, scales[:4])
    put_scales(second_ref, scales[4:])


def apply_kernel(in_ref, w_ref, out_ref):
    scales = []
    for s in range(8):
        first = s // 4 * 12 + s % 4 * 2
        x0, x1, g = in_ref[:, at(first)], in_ref[:, at(first + 1)], in_ref[:, at(s // 4 * 12 + 8 + s % 4)]
        w0, w1 = w_ref[2 * s], w_ref[2 * s + 1]
        values = (
            dot(x0, w0, ((1,), (0,))) + dot(x1, w1, ((1,), (0,))),
            dot(g, w0, ((1,), (1,))),
            dot(g, w1, ((1,), (1,))),
        )
        for slot, value in enumerate(values):
            q, e = fixed(value)
            out_ref[:, at(3 * s + slot)] = q
            scales.append(e)
    put_scales(out_ref, scales)


def here(*arrays):
    return [pltpu.with_memory_space_constraint(a, pltpu.VMEM) for a in arrays]


def vmem(n):
    return [pl.BlockSpec(memory_space=pltpu.VMEM)] * n


PART = 8 * B + SCALES


def grad(received, other, after):
    return pl.pallas_call(
        grad_kernel,
        out_shape=[pltpu.VMEM((128, 4 * B + SCALES), jnp.int16)] * 2 + [pltpu.VMEM((128, 8 * B), jnp.float32)],
        in_specs=vmem(2) + [ANY],
        out_specs=vmem(3),
        scratch_shapes=[pltpu.VMEM((16, 2, S, B), jnp.float32)],
        compiler_params=ROOM,
        name="grad",
    )(*here(received, other), after)


def half_kernel(in_ref, out_ref):
    theirs = 1 - position()[0]
    for j in range(12):
        out_ref[:, at(j)] = in_ref[:, pl.ds(pl.multiple_of(theirs * HALF + j * B, B), B)]


def half(received):
    return pl.pallas_call(
        half_kernel,
        out_shape=pltpu.VMEM((OWNERS * S, HALF), jnp.bfloat16),
        in_specs=vmem(1),
        out_specs=vmem(1)[0],
        compiler_params=ROOM,
        name="half",
    )(*here(received))


def apply(received, blocks):
    return pl.pallas_call(
        apply_kernel,
        out_shape=jax.ShapeDtypeStruct((OWNERS * S, MESSAGE + SCALES), jnp.int16),
        in_specs=vmem(2),
        compiler_params=ROOM,
        cost_estimate=pl.CostEstimate(flops=5_000_000_000, bytes_accessed=20_000_000, transcendentals=0),
        name="apply",
    )(*here(received, blocks))


def pairs_kernel(keep_ref, first_ref, second_ref, *refs):
    outs, own_ref, total_ref = refs[:3], refs[3], refs[4]
    pair = position()[1] // 2
    got = (first_ref, second_ref)
    before = [decoded(ref[:, 4 * B :]) for ref in got]
    scales = [[] for _ in range(3)]
    for j in range(8):
        i = j % 4
        total = keep_ref[:, at(j)] + widened(got[j // 4][:, at(i)]) * before[j // 4][:, i : i + 1]
        total_ref[...] = total.reshape(XL, 4, S, B)
        own_ref[:, at(j)] = total_ref[:, pl.ds(pair, 1)].reshape(32, B)
        for d in range(3):
            q, e = fixed(total_ref[:, pl.ds(lax.rem(pair + PAIR_STEPS[d], 4), 1)].reshape(32, B))
            outs[d][:, at(j)] = q
            scales[d].append(e)
    for d in range(3):
        put_scales(outs[d], scales[d])


def pairs(keep, first, second):
    return pl.pallas_call(
        pairs_kernel,
        out_shape=[pltpu.VMEM((32, PART), jnp.int16)] * 3
        + [pltpu.VMEM((32, 8 * B), jnp.float32)],
        in_specs=vmem(3),
        out_specs=vmem(4),
        scratch_shapes=[pltpu.VMEM((XL, 4, S, B), jnp.float32)],
        compiler_params=ROOM,
        cost_estimate=LONG,
        name="pairs",
    )(*here(keep, first, second))


def cut_kernel(own_ref, a_ref, b_ref, c_ref, *refs):
    outs, keep_ref, total_ref = refs[:3], refs[3], refs[4]
    xl = position()[2]
    ins = (a_ref, b_ref, c_ref)
    before = [decoded(ref[:, 8 * B :]) for ref in ins]
    scales = [[] for _ in range(3)]
    for j in range(8):
        total = own_ref[:, at(j)]
        for ref, scale in zip(ins, before):
            total = total + widened(ref[:, at(j)]) * scale[:, j : j + 1]
        total_ref[...] = total.reshape(XL, S, B)
        keep_ref[:, at(j)] = total_ref[xl]
        for d in range(3):
            q, e = fixed(total_ref[xl ^ (d + 1)])
            outs[d][:, at(j)] = q
            scales[d].append(e)
    for d in range(3):
        put_scales(outs[d], scales[d])


def cut(own, parts):
    return pl.pallas_call(
        cut_kernel,
        out_shape=[pltpu.VMEM((S, PART), jnp.int16)] * 3 + [pltpu.VMEM((S, 8 * B), jnp.float32)],
        in_specs=vmem(4),
        out_specs=vmem(4),
        scratch_shapes=[pltpu.VMEM((XL, S, B), jnp.float32)],
        compiler_params=ROOM,
        name="cut",
    )(*here(own, *parts))


def last_kernel(own_ref, a_ref, b_ref, c_ref, mine_ref, send_ref):
    ins = (a_ref, b_ref, c_ref)
    scales = [decoded(ref[:, 8 * B :]) for ref in ins]
    first = position()[0] == 0
    for j in range(8):
        total = own_ref[:, at(j)]
        for ref, scale in zip(ins, scales):
            total = total + widened(ref[:, at(j)]) * scale[:, j : j + 1]
        total = total * 8192.0**-0.5
        top, bottom = total[:4], total[4:]
        mine_ref[j] = jnp.where(first, top, bottom)
        send_ref[j] = jnp.where(first, bottom, top)


def last(own, parts):
    return pl.pallas_call(
        last_kernel,
        out_shape=[pltpu.VMEM((8, 4, B), jnp.float32)] * 2,
        in_specs=vmem(4),
        out_specs=vmem(2),
        compiler_params=ROOM,
        name="last",
    )(*here(own, *parts))


def place_kernel(cols, rows, in_ref, out_ref, grad_ref, mark_ref, first_ref, second_ref):
    mark_ref[...] = jnp.zeros_like(mark_ref)
    totals = (first_ref, second_ref)
    for ref in totals:
        ref[...] = jnp.zeros_like(ref)

    @pl.loop(0, OWNERS, unroll=8)
    def _(p):
        scale = decoded(in_ref[p, :, MESSAGE:])
        values = [widened(in_ref[p, :, at(j)]) * scale[:, j : j + 1] for j in range(24)]
        for s in range(8):
            row = pl.multiple_of(rows[p * 16 + 2 * s] * B, B)
            out_ref[:, pl.ds(row, B)] = values[3 * s].astype(jnp.bfloat16)
            for member, ref in enumerate(totals):
                col = pl.multiple_of(cols[p * 16 + 2 * s + member] * B, B)
                ref[:, pl.ds(col, B)] += values[3 * s + 1 + member]

    grad_ref[...] = (first_ref[...] + second_ref[...]).astype(jnp.bfloat16)


def place(block_cols, block_rows, back):
    return pl.pallas_call(
        place_kernel,
        out_shape=[jax.ShapeDtypeStruct((S, 128 * B), jnp.bfloat16)] * 2 + [pltpu.VMEM((S, 128), jnp.float32)],
        in_specs=[SMEM, SMEM] + vmem(1),
        scratch_shapes=[pltpu.VMEM((S, 128 * B), jnp.float32)] * 2,
        compiler_params=ROOM,
        name="place",
    )(block_cols, block_rows, *here(back))


def join_kernel(mine_ref, swapped_ref, after_ref, out_ref):
    first = position()[0] == 0
    mine, swapped = mine_ref[...], swapped_ref[...]
    out_ref[:8] = jnp.where(first, mine, swapped)
    out_ref[8:] = jnp.where(first, swapped, mine)


def join(mine, swapped, after):
    return pl.pallas_call(
        join_kernel,
        out_shape=jax.ShapeDtypeStruct((16, 4, B), jnp.float32),
        in_specs=vmem(3),
        compiler_params=ROOM,
        name="join",
    )(*here(mine, swapped, after))


def shards(shots_in, cotangent, blocks, block_rows, block_cols):
    permute = functools.partial(lax.ppermute, axis_name=AXES)
    exchange = functools.partial(
        lax.all_to_all, axis_name=AXES, split_axis=0, concat_axis=0, axis_index_groups=groups(), tiled=True
    )

    received = exchange(gather(block_cols, block_rows, shots_in, cotangent)).reshape(OWNERS * S, MESSAGE)
    other = permute(half(received), perm=moves(lambda a, b, c: (a, b, 1 - c)))
    result = apply(received, blocks)
    first, second, keep = grad(received, other, result)
    first = permute(first, perm=moves(lambda a, b, c: (a, b ^ 1, c)))
    second = permute(second, perm=moves(lambda a, b, c: (a, ((b + 1) ^ 1) - 1 & 7, c)))
    back = exchange(result.reshape(OWNERS, S, MESSAGE + SCALES))
    *parts, own = pairs(keep, first, second)
    parts = [
        permute(part, perm=moves(lambda a, b, c, d=d: (a, (b + 2 * d) % Y, c))) for d, part in zip(PAIR_STEPS, parts)
    ]
    *parts, own = cut(own, parts)
    parts = [
        permute(part, perm=moves(lambda a, b, c, d=d: (a ^ (d + 1), b, c))) for d, part in enumerate(parts)
    ]
    mine, send = last(own, parts)
    swapped = permute(send, perm=moves(lambda a, b, c: (a, b, 1 - c)))
    shots_out, input_grad, placed = place(block_cols, block_rows, back)
    weight_grad = join(mine, swapped, placed)
    return shots_out, input_grad, weight_grad


def solution(mesh):
    return jax.shard_map(
        shards,
        mesh=mesh,
        in_specs=(P(AXES, None), P(AXES, None), P("fsdp", None, None), P(), P()),
        out_specs=(P(AXES, None), P(AXES, None), P("fsdp", "dp", None)),
        check_vma=False,
    )
```

```python
import functools

import jax
import jax.numpy as jnp
from jax import lax
from jax.experimental import pallas as pl
from jax.experimental.pallas import tpu as pltpu
from jax.sharding import PartitionSpec as P

AXES = ("dp", "fsdp")
XL, Y, CORES, XH, Z = 4, 8, 2, 2, 8
OWNERS = XH * Z
S = 8
B = 256
HALF = 12 * B
MESSAGE = 2 * HALF
SCALES = 128
STEPS = 16.0
PAIR_STEPS = (2, 1, 3)
SMEM = pl.BlockSpec(memory_space=pltpu.SMEM)
ANY = pl.BlockSpec(memory_space=pl.ANY)
ROOM = pltpu.CompilerParams(vmem_limit_bytes=24 * 2**20)


def device(xl, y, core, xh, z):
    return (((xl * Y + y) * CORES + core) * XH + xh) * Z + z


def position():
    dp = lax.axis_index("dp")
    return lax.rem(dp, CORES), lax.rem(lax.div(dp, CORES), Y), lax.div(dp, CORES * Y)


def groups():
    return [
        [device((xl + 2 * xh) % XL, y, core, xh, z) for xh in range(XH) for z in range(Z)]
        for xl in range(XL)
        for y in range(Y)
        for core in range(CORES)
    ]


def moves(target):
    return [
        (device(xl, y, core, xh, z), device(*target(xl, y, core), xh, z))
        for xl in range(XL)
        for y in range(Y)
        for core in range(CORES)
        for xh in range(XH)
        for z in range(Z)
    ]


LONG = pl.CostEstimate(flops=80_000_000_000, bytes_accessed=1_000_000, transcendentals=0)


def gather_kernel(cols, rows, x_hbm, g_hbm, out_hbm, x_ref, g_ref, out_ref, in_sems, out_sems):
    loads = [
        pltpu.make_async_copy(x_hbm, x_ref, in_sems.at[0]),
        pltpu.make_async_copy(g_hbm, g_ref, in_sems.at[1]),
    ]
    for load in loads:
        load.start()
    for load in loads:
        load.wait()
    stores = []
    for chunk in range(4):
        owners = slice(chunk * 4, chunk * 4 + 4)
        for p in range(owners.start, owners.stop):
            for half in range(2):
                first = p * 16 + half * 8
                for j in range(8):
                    col = pl.multiple_of(cols[first + j] * B, B)
                    out_ref[p, :, at(half * 12 + j)] = x_ref[:, pl.ds(col, B)]
                for j in range(4):
                    row = pl.multiple_of(rows[first + 2 * j] * B, B)
                    out_ref[p, :, at(half * 12 + 8 + j)] = g_ref[:, pl.ds(row, B)]
        stores.append(pltpu.make_async_copy(out_ref.at[owners], out_hbm.at[owners], out_sems.at[chunk]))
        stores[-1].start()
    for store in stores:
        store.wait()


def gather(block_cols, block_rows, shots_in, cotangent):
    message = (OWNERS, S, MESSAGE)
    return pl.pallas_call(
        gather_kernel,
        out_shape=jax.ShapeDtypeStruct(message, jnp.bfloat16),
        in_specs=[SMEM, SMEM, ANY, ANY],
        out_specs=ANY,
        scratch_shapes=[pltpu.VMEM((S, 128 * B), jnp.bfloat16)] * 2
        + [
            pltpu.VMEM(message, jnp.bfloat16),
            pltpu.SemaphoreType.DMA((2,)),
            pltpu.SemaphoreType.DMA((4,)),
        ],
        name="gather",
    )(block_cols, block_rows, shots_in, cotangent)


def fixed(v):
    top = jnp.max(jnp.abs(v), axis=1, keepdims=True)
    e = jnp.ceil(jnp.log2(jnp.maximum(top, 2.0**-120)) * STEPS + 0.01)
    return jnp.round(v * (jnp.exp2(e * (-1.0 / STEPS)) * 32760.0)).astype(jnp.int32).astype(jnp.int16), e


def decoded(e):
    return jnp.exp2(e.astype(jnp.int32).astype(jnp.float32) * (1.0 / STEPS)) * (1.0 / 32760.0)


def widened(q):
    return q.astype(jnp.int32).astype(jnp.float32)


def at(j, width=B):
    return slice(j * B, j * B + width)


def dot(u, v, over):
    return lax.dot_general(u, v, (over, ((), ())), preferred_element_type=jnp.float32)


def put_scales(ref, scales):
    lanes = lax.broadcasted_iota(jnp.int32, (scales[0].shape[0], SCALES), 1)
    out = jnp.zeros(lanes.shape, jnp.float32)
    for j, e in enumerate(scales):
        out = jnp.where(lanes == j, e, out)
    ref[:, ref.shape[1] - SCALES :] = out.astype(jnp.int32).astype(jnp.int16)


def grad_kernel(in_ref, other_ref, after_ref, first_ref, second_ref, keep_ref, wg_ref):
    core, y, _ = position()
    parity = y % 2
    scales = []
    for j in range(8):
        own = lambda slot: in_ref[:, pl.ds(pl.multiple_of(core * HALF + slot * B, B), B)]
        x0, g0 = own(j), own(8 + j // 2)
        x1, g1 = other_ref[:, at(j)], other_ref[:, at(8 + j // 2)]
        wg = dot(x0, g0, ((0,), (0,))) + dot(x1, g1, ((0,), (0,)))
        wg_ref[...] = wg.reshape(16, 2, S, B)
        keep_ref[:, at(j)] = wg_ref[:, pl.ds(parity, 1)].reshape(128, B)
        q, e = fixed(wg_ref[:, pl.ds(1 - parity, 1)].reshape(128, B))
        (first_ref, second_ref)[j // 4][:, at(j % 4)] = q
        scales.append(e)
    put_scales(first_ref, scales[:4])
    put_scales(second_ref, scales[4:])


def apply_kernel(in_ref, w_ref, out_ref):
    scales = []
    for s in range(8):
        first = s // 4 * 12 + s % 4 * 2
        x0, x1, g = in_ref[:, at(first)], in_ref[:, at(first + 1)], in_ref[:, at(s // 4 * 12 + 8 + s % 4)]
        w0, w1 = w_ref[2 * s], w_ref[2 * s + 1]
        values = (
            dot(x0, w0, ((1,), (0,))) + dot(x1, w1, ((1,), (0,))),
            dot(g, w0, ((1,), (1,))),
            dot(g, w1, ((1,), (1,))),
        )
        for slot, value in enumerate(values):
            q, e = fixed(value)
            out_ref[:, at(3 * s + slot)] = q
            scales.append(e)
    put_scales(out_ref, scales)


def here(*arrays):
    return [pltpu.with_memory_space_constraint(a, pltpu.VMEM) for a in arrays]


def vmem(n):
    return [pl.BlockSpec(memory_space=pltpu.VMEM)] * n


PART = 8 * B + SCALES


def grad(received, other, after):
    return pl.pallas_call(
        grad_kernel,
        out_shape=[pltpu.VMEM((128, 4 * B + SCALES), jnp.int16)] * 2 + [pltpu.VMEM((128, 8 * B), jnp.float32)],
        in_specs=vmem(2) + [ANY],
        out_specs=vmem(3),
        scratch_shapes=[pltpu.VMEM((16, 2, S, B), jnp.float32)],
        compiler_params=ROOM,
        name="grad",
    )(*here(received, other), after)


def half_kernel(in_ref, out_ref):
    theirs = 1 - position()[0]
    for j in range(12):
        out_ref[:, at(j)] = in_ref[:, pl.ds(pl.multiple_of(theirs * HALF + j * B, B), B)]


def half(received):
    return pl.pallas_call(
        half_kernel,
        out_shape=pltpu.VMEM((OWNERS * S, HALF), jnp.bfloat16),
        in_specs=vmem(1),
        out_specs=vmem(1)[0],
        compiler_params=ROOM,
        name="half",
    )(*here(received))


def apply(received, blocks):
    return pl.pallas_call(
        apply_kernel,
        out_shape=jax.ShapeDtypeStruct((OWNERS * S, MESSAGE + SCALES), jnp.int16),
        in_specs=vmem(2),
        compiler_params=ROOM,
        cost_estimate=pl.CostEstimate(flops=5_000_000_000, bytes_accessed=20_000_000, transcendentals=0),
        name="apply",
    )(*here(received, blocks))


def pairs_kernel(keep_ref, first_ref, second_ref, *refs):
    outs, own_ref, total_ref = refs[:3], refs[3], refs[4]
    pair = position()[1] // 2
    got = (first_ref, second_ref)
    before = [decoded(ref[:, 4 * B :]) for ref in got]
    scales = [[] for _ in range(3)]
    for j in range(8):
        i = j % 4
        total = keep_ref[:, at(j)] + widened(got[j // 4][:, at(i)]) * before[j // 4][:, i : i + 1]
        total_ref[...] = total.reshape(XL, 4, S, B)
        own_ref[:, at(j)] = total_ref[:, pl.ds(pair, 1)].reshape(32, B)
        for d in range(3):
            q, e = fixed(total_ref[:, pl.ds(lax.rem(pair + PAIR_STEPS[d], 4), 1)].reshape(32, B))
            outs[d][:, at(j)] = q
            scales[d].append(e)
    for d in range(3):
        put_scales(outs[d], scales[d])


def pairs(keep, first, second):
    return pl.pallas_call(
        pairs_kernel,
        out_shape=[pltpu.VMEM((32, PART), jnp.int16)] * 3
        + [pltpu.VMEM((32, 8 * B), jnp.float32)],
        in_specs=vmem(3),
        out_specs=vmem(4),
        scratch_shapes=[pltpu.VMEM((XL, 4, S, B), jnp.float32)],
        compiler_params=ROOM,
        cost_estimate=LONG,
        name="pairs",
    )(*here(keep, first, second))


def cut_kernel(own_ref, a_ref, b_ref, c_ref, *refs):
    outs, keep_ref, total_ref = refs[:3], refs[3], refs[4]
    xl = position()[2]
    ins = (a_ref, b_ref, c_ref)
    before = [decoded(ref[:, 8 * B :]) for ref in ins]
    scales = [[] for _ in range(3)]
    for j in range(8):
        total = own_ref[:, at(j)]
        for ref, scale in zip(ins, before):
            total = total + widened(ref[:, at(j)]) * scale[:, j : j + 1]
        total_ref[...] = total.reshape(XL, S, B)
        keep_ref[:, at(j)] = total_ref[xl]
        for d in range(3):
            q, e = fixed(total_ref[xl ^ (d + 1)])
            outs[d][:, at(j)] = q
            scales[d].append(e)
    for d in range(3):
        put_scales(outs[d], scales[d])


def cut(own, parts):
    return pl.pallas_call(
        cut_kernel,
        out_shape=[pltpu.VMEM((S, PART), jnp.int16)] * 3 + [pltpu.VMEM((S, 8 * B), jnp.float32)],
        in_specs=vmem(4),
        out_specs=vmem(4),
        scratch_shapes=[pltpu.VMEM((XL, S, B), jnp.float32)],
        compiler_params=ROOM,
        name="cut",
    )(*here(own, *parts))


def last_kernel(own_ref, a_ref, b_ref, c_ref, mine_ref, send_ref):
    ins = (a_ref, b_ref, c_ref)
    scales = [decoded(ref[:, 8 * B :]) for ref in ins]
    first = position()[0] == 0
    for j in range(8):
        total = own_ref[:, at(j)]
        for ref, scale in zip(ins, scales):
            total = total + widened(ref[:, at(j)]) * scale[:, j : j + 1]
        total = total * 8192.0**-0.5
        top, bottom = total[:4], total[4:]
        mine_ref[j] = jnp.where(first, top, bottom)
        send_ref[j] = jnp.where(first, bottom, top)


def last(own, parts):
    return pl.pallas_call(
        last_kernel,
        out_shape=[pltpu.VMEM((8, 4, B), jnp.float32)] * 2,
        in_specs=vmem(4),
        out_specs=vmem(2),
        compiler_params=ROOM,
        name="last",
    )(*here(own, *parts))


def place_kernel(cols, rows, in_ref, out_ref, grad_ref, mark_ref, first_ref, second_ref):
    mark_ref[...] = jnp.zeros_like(mark_ref)
    totals = (first_ref, second_ref)
    for ref in totals:
        ref[...] = jnp.zeros_like(ref)

    @pl.loop(0, OWNERS, unroll=8)
    def _(p):
        scale = decoded(in_ref[p, :, MESSAGE:])
        values = [widened(in_ref[p, :, at(j)]) * scale[:, j : j + 1] for j in range(24)]
        for s in range(8):
            row = pl.multiple_of(rows[p * 16 + 2 * s] * B, B)
            out_ref[:, pl.ds(row, B)] = values[3 * s].astype(jnp.bfloat16)
            for member, ref in enumerate(totals):
                col = pl.multiple_of(cols[p * 16 + 2 * s + member] * B, B)
                ref[:, pl.ds(col, B)] += values[3 * s + 1 + member]

    grad_ref[...] = (first_ref[...] + second_ref[...]).astype(jnp.bfloat16)


def place(block_cols, block_rows, back):
    return pl.pallas_call(
        place_kernel,
        out_shape=[jax.ShapeDtypeStruct((S, 128 * B), jnp.bfloat16)] * 2 + [pltpu.VMEM((S, 128), jnp.float32)],
        in_specs=[SMEM, SMEM] + vmem(1),
        scratch_shapes=[pltpu.VMEM((S, 128 * B), jnp.float32)] * 2,
        compiler_params=ROOM,
        name="place",
    )(block_cols, block_rows, *here(back))


def join_kernel(mine_ref, swapped_ref, after_ref, out_ref):
    first = position()[0] == 0
    mine, swapped = mine_ref[...], swapped_ref[...]
    out_ref[:8] = jnp.where(first, mine, swapped)
    out_ref[8:] = jnp.where(first, swapped, mine)


def join(mine, swapped, after):
    return pl.pallas_call(
        join_kernel,
        out_shape=jax.ShapeDtypeStruct((16, 4, B), jnp.float32),
        in_specs=vmem(3),
        compiler_params=ROOM,
        name="join",
    )(*here(mine, swapped, after))


def shards(shots_in, cotangent, blocks, block_rows, block_cols):
    permute = functools.partial(lax.ppermute, axis_name=AXES)
    exchange = functools.partial(
        lax.all_to_all, axis_name=AXES, split_axis=0, concat_axis=0, axis_index_groups=groups(), tiled=True
    )

    received = exchange(gather(block_cols, block_rows, shots_in, cotangent)).reshape(OWNERS * S, MESSAGE)
    other = permute(half(received), perm=moves(lambda a, b, c: (a, b, 1 - c)))
    result = apply(received, blocks)
    first, second, keep = grad(received, other, result)
    first = permute(first, perm=moves(lambda a, b, c: (a, b ^ 1, c)))
    second = permute(second, perm=moves(lambda a, b, c: (a, ((b + 1) ^ 1) - 1 & 7, c)))
    back = exchange(result.reshape(OWNERS, S, MESSAGE + SCALES))
    *parts, own = pairs(keep, first, second)
    parts = [
        permute(part, perm=moves(lambda a, b, c, d=d: (a, (b + 2 * d) % Y, c))) for d, part in zip(PAIR_STEPS, parts)
    ]
    *parts, own = cut(own, parts)
    parts = [
        permute(part, perm=moves(lambda a, b, c, d=d: (a ^ (d + 1), b, c))) for d, part in reversed(list(enumerate(parts)))
    ]
    mine, send = last(own, parts)
    swapped = permute(send, perm=moves(lambda a, b, c: (a, b, 1 - c)))
    shots_out, input_grad, placed = place(block_cols, block_rows, back)
    weight_grad = join(mine, swapped, placed)
    return shots_out, input_grad, weight_grad


def solution(mesh):
    return jax.shard_map(
        shards,
        mesh=mesh,
        in_specs=(P(AXES, None), P(AXES, None), P("fsdp", None, None), P(), P()),
        out_specs=(P(AXES, None), P(AXES, None), P("fsdp", "dp", None)),
        check_vma=False,
    )
```
